512 devices in a mesh: queue: 64 (over z, y_lo, x), space: 8 (over y_hi, core).
Axes of the slice: x: 4, y: 8 (y_hi: 4, y_lo: 2; y = y_hi * 2 + y_lo), z: 8, core: 2. Of those that a mesh axis runs over, the one named last changes fastest.
Arguments:
- queries: bfloat16 [64, 1024, 1536], P('queue', 'space'), as said below
- keys: bfloat16 [64, 1024, 1536], P('queue', 'space'), as said below
- values: bfloat16 [64, 1024, 1536], P('queue', 'space'), may hold values from -6 to 6
- levels: int32 [64], P('queue'), may hold values from 0 to 63
- plan: int32 [64], replicated, may hold values from 0 to 127
- gate_table: float32 [128, 1536], replicated, may hold values from -5 to 5
- fresh: bfloat16 [1024, 1536], P('space'), may hold values from -6 to 6
Outputs:
- denoised: bfloat16 [64, 1024, 1536], P('queue', 'space')
- queue_next: bfloat16 [64, 1024, 1536], P('queue', 'space')
The draws below stay inside these ranges and needn't reach their ends.
Inputs may be any that keep to these rules, and one draw needn't show every extreme that they name: Most keys are of order one; a few key rows may nearly equal a neighbouring key row of the same frame. Most queries are of order one; a few query rows may be up to 40 times a key row of the same frame, so that single scores can reach a few hundred.
All inputs are finite; a program needn't handle non-finite values.
Results may differ from the reference program's by a relative error of at most 0.0057.
Values may be sent and summed in bfloat16 or wider, within the bound.
A program may use at most 64 MiB of HBM per device.

```python
import jax
import jax.numpy as jnp
from jax import lax

HEADS = 24
HEAD_SIZE = 64
STEPS = 128
FRAMES = 64
LEVELS = 64
TOKENS_FRAME = 1024
HD = 1536


def base_keys(key):
    return jax.random.normal(key, (FRAMES, TOKENS_FRAME, HD), jnp.float32)


def draw_keys(key, part):
    shared = base_keys(key)
    result = shared
    return result.astype(jnp.bfloat16)


def draw_queries(key, part):
    key = jax.random.fold_in(key, 23)
    first_key = jax.random.fold_in(key, 0)
    result = jax.random.normal(first_key, (FRAMES, TOKENS_FRAME, HD), jnp.float32)
    return result.astype(jnp.bfloat16)


def with_ends(entries, stream_key, least, top_value):
    longest = entries.shape.index(max(entries.shape))
    spots = []
    for shift in (0, 1):
        where = [jax.random.randint(jax.random.fold_in(stream_key, axis), (), 0, length) for axis, length in enumerate(entries.shape)]
        where[longest] = (where[longest] + shift) % entries.shape[longest]
        spots.append(tuple(where))
    return entries.at[spots[0]].set(least).at[spots[1]].set(top_value)


def block_scale(own_key, extent, cuts, least, largest):
    loudness, own = 1.0, jax.random.fold_in(own_key, 6)
    for dim, parts in cuts:
        draws = jnp.exp(jax.random.uniform(jax.random.fold_in(own, dim), (parts,), jnp.float32, least / len(cuts), largest / len(cuts)))
        loudness = loudness * jnp.repeat(draws, extent[dim] // parts).reshape([-1 if axis == dim else 1 for axis in range(len(extent))])
    return loudness


def normal_values(own_key, extent, deviation, bound, cuts=(), held_as=jnp.bfloat16):
    factor_of = block_scale(own_key, extent, cuts, -0.22, 0.18) if cuts else 1.0
    entries = jax.random.normal(own_key, extent, jnp.float32) * deviation * factor_of
    return jnp.minimum(jnp.maximum(entries, -bound), bound).astype(held_as)


def setup_inputs(seed: int = 0) -> dict:
    splits = jax.random.split(jax.random.key(seed), 8)
    return {
        "queries": draw_queries(jax.random.fold_in(splits[7], 71), 0),
        "keys": draw_keys(jax.random.fold_in(splits[7], 71), 0),
        "values": normal_values(splits[2], (FRAMES, TOKENS_FRAME, HD), 1.0, 6.0, ((0, 64), (1, 8))),
        "levels": with_ends(jax.random.randint(splits[3], (FRAMES,), 0, LEVELS), jax.random.fold_in(splits[3], 1), 0, LEVELS - 1).astype(jnp.int32),
        "plan": with_ends(jax.random.randint(splits[4], (LEVELS,), 0, STEPS), jax.random.fold_in(splits[4], 1), 0, STEPS - 1).astype(jnp.int32),
        "gate_table": normal_values(splits[5], (STEPS, HD), 1.0, 5.0, (), jnp.float32),
        "fresh": normal_values(splits[6], (TOKENS_FRAME, HD), 1.0, 6.0, ((0, 8),)),
    }


def reference(queries, keys, values, levels, plan, gate_table, fresh):
    zero_frame = jnp.zeros_like(keys[:1])
    keys_prev = jnp.concatenate([zero_frame, keys[:-1]], 0)
    values_prev = jnp.concatenate([zero_frame, values[:-1]], 0)
    first_flag = jnp.arange(FRAMES) == 0
    halo_col = jnp.arange(2 * TOKENS_FRAME) >= TOKENS_FRAME

    def one_frame(inputs):
        query, key_own, value_own, key_prev, value_prev, flag = inputs
        query_heads = query.astype(jnp.float32).reshape(TOKENS_FRAME, HEADS, HEAD_SIZE)
        key_all = jnp.concatenate([key_own, key_prev], 0).astype(jnp.float32).reshape(2 * TOKENS_FRAME, HEADS, HEAD_SIZE)
        value_all = jnp.concatenate([value_own, value_prev], 0).astype(jnp.float32).reshape(2 * TOKENS_FRAME, HEADS, HEAD_SIZE)
        scores = jnp.einsum("qhd,khd->hqk", query_heads, key_all) * (HEAD_SIZE ** -0.5)
        scores = jnp.where(flag & halo_col[None, None, :], -jnp.inf, scores)
        top = jnp.max(scores, axis=-1, keepdims=True)
        expo = jnp.exp(scores - top)
        total = jnp.sum(expo, axis=-1)
        probs = lax.optimization_barrier(expo.astype(jnp.bfloat16)).astype(jnp.float32)
        mixed = jnp.einsum("hqk,khd->qhd", probs, value_all) / jnp.swapaxes(total, 0, 1)[:, :, None]
        return mixed.reshape(TOKENS_FRAME, HD).astype(jnp.bfloat16)

    attn = lax.map(one_frame, (queries, keys, values, keys_prev, values_prev, first_flag))
    step_index = plan[levels]
    gate = gate_table[step_index]
    denoised = (gate[:, None, :] * attn.astype(jnp.float32)).astype(jnp.bfloat16)
    queue_next = jnp.concatenate([denoised[1:], fresh[None]], 0)
    return denoised, queue_next
```

```python
import functools

import jax
import jax.numpy as jnp
from jax import lax
from jax.experimental import pallas as pl
from jax.experimental.pallas import tpu as pltpu
from jax.sharding import PartitionSpec as P

MESH = pl.DeviceIdType.MESH
BF16 = jnp.bfloat16
F32 = jnp.float32
ROWS = 128
HALF = 64
COLS = 1536
GROUPS = 8
FAR_FIRST = (4, 3, 5, 2, 6, 1, 7, 0)
PAIR_ORDER = (2, 1, 3, 0)
K, V, Q = 0, 1, 2


def dot_nt(a, b):
    return lax.dot_general(a, b, (((1,), (1,)), ((), ())), preferred_element_type=F32)


def left_lanes(shape):
    return lax.broadcasted_iota(jnp.int32, shape, len(shape) - 1) < HALF


def swap_halves(a):
    return pltpu.roll(a.astype(F32), HALF, a.ndim - 1).astype(a.dtype)


def tile_of(group):
    return 3 * (group // 2) + 2 * (group % 2)


def columns(tile):
    return pl.ds(pl.multiple_of(tile * 128, 128), 128)


def kernel(
    q_hbm, k_hbm, v_hbm, levels_ref, plan_ref, gate_hbm, fresh_hbm,
    den_ref, next_ref,
    src, packed, gate_buf,
    kt, vt, qt, kh, vh, qh,
    va, vb, ha, hb,
    ot, oh, ort, orh,
    in_sem, gate_sem,
    send_t, recv_t, send_h, recv_h,
    fwd_send_t, fwd_recv_t, fwd_send_h, fwd_recv_h,
    o_send_t, o_recv_t, o_send_h, o_recv_h,
    shift_send, shift_recv, fresh_sem,
):
    queue = lax.axis_index("queue")
    space = lax.axis_index("space")
    z, y_lo, x = queue // 8, (queue // 4) % 2, queue % 4
    y_hi, core = space // 2, space % 2
    y = y_hi * 2 + y_lo
    frame = z * 8 + core * 4 + x
    tokens_in = (kt, vt, qt)
    heads_in = (kh, vh, qh)

    def worker(of_frame, group):
        return (
            (of_frame // 8) * 8 + (group % 2) * 4 + of_frame % 4,
            (group // 2) * 2 + (of_frame // 4) % 2,
        )

    loads = [
        pltpu.make_async_copy(ref.at[0], src.at[i], in_sem.at[i])
        for i, ref in enumerate((k_hbm, v_hbm, q_hbm))
    ]
    for load in loads:
        load.start()
    gate_load = pltpu.make_async_copy(gate_hbm, gate_buf, gate_sem)
    gate_load.start()

    barrier = pltpu.get_barrier_semaphore()

    def greet(device):
        pl.semaphore_signal(barrier, inc=1, device_id=device, device_id_type=MESH)

    has_prev, has_next = frame > 0, frame < 63
    has_ahead, has_behind = queue > 0, queue < 63
    owns = core == y_lo
    for i in range(8):
        @pl.when(jnp.logical_not(owns & (space == i)))
        def _():
            greet((frame, i))
    pl.when(has_prev)(lambda: greet(worker(frame - 1, y)))
    pl.when(has_behind)(lambda: greet((queue + 1, space)))
    for i in range(GROUPS):
        @pl.when(jnp.logical_not(owns & (y == i)))
        def _():
            greet(worker(queue, i))
    greeted = (
        16
        - 2 * owns.astype(jnp.int32)
        + has_next.astype(jnp.int32)
        + has_ahead.astype(jnp.int32)
    )

    def pack(i):
        left = left_lanes((HALF, 128))
        for pair in range(4):
            tile = src[i, :, (3 * pair + 1) * 128 : (3 * pair + 2) * 128]
            top, bottom = tile[:HALF], tile[HALF:]
            packed[i, 2 * pair] = jnp.where(left, top, swap_halves(bottom))
            packed[i, 2 * pair + 1] = jnp.where(left, swap_halves(top), bottom)

    for i in (K, V, Q):
        loads[i].wait()
        pack(i)
    pl.semaphore_wait(barrier, greeted)

    def rows_of(index, size):
        return pl.ds(pl.multiple_of(index * size, size), size)

    def sent_tile(i, group):
        return pltpu.make_async_remote_copy(
            src_ref=src.at[i, :, columns(tile_of(group))],
            dst_ref=tokens_in[i].at[rows_of(space, ROWS)],
            send_sem=send_t.at[i, group], recv_sem=recv_t.at[i, space],
            device_id=worker(queue, group), device_id_type=MESH,
        )

    def sent_head(i, group):
        return pltpu.make_async_remote_copy(
            src_ref=packed.at[i, group],
            dst_ref=heads_in[i].at[rows_of(space, HALF)],
            send_sem=send_h.at[i, group], recv_sem=recv_h.at[i, space],
            device_id=worker(queue, group), device_id_type=MESH,
        )

    def send_out(make, kept, i):
        for shift in FAR_FIRST:
            group = (y + shift) % GROUPS
            if shift:
                make(i, group).start()
            else:
                pl.when(owns)(lambda: kept(i).start())
                pl.when(jnp.logical_not(owns))(lambda: make(i, group).start())

    def kept_tile(i):
        return pltpu.make_async_copy(
            src.at[i, :, columns(tile_of(y))],
            tokens_in[i].at[rows_of(space, ROWS)],
            recv_t.at[i, space],
        )

    def kept_head(i):
        return pltpu.make_async_copy(
            packed.at[i, y],
            heads_in[i].at[rows_of(space, HALF)],
            recv_h.at[i, space],
        )

    with jax.named_scope("send_all"):
        for i in (K, V, Q):
            send_out(sent_tile, kept_tile, i)
        for i in (K, V, Q):
            send_out(sent_head, kept_head, i)

    def arrival_tile(i, shard):
        return pltpu.make_async_copy(
            tokens_in[i].at[rows_of(shard, ROWS)], tokens_in[i].at[rows_of(shard, ROWS)], recv_t.at[i, shard]
        )

    def arrival_head(i, shard):
        return pltpu.make_async_copy(
            heads_in[i].at[rows_of(shard, HALF)], heads_in[i].at[rows_of(shard, HALF)], recv_h.at[i, shard]
        )

    def forward(buf, i, pair, size, sends, recvs):
        return pltpu.make_async_remote_copy(
            src_ref=buf.at[rows_of(pair, 2 * size)],
            dst_ref=buf.at[rows_of(4 + pair, 2 * size)],
            send_sem=sends.at[i, pair], recv_sem=recvs.at[i, pair],
            device_id=worker(frame + 1, y), device_id_type=MESH,
        )

    def own_pair(arrival, i, pair):
        arrival(i, 2 * pair).wait()
        arrival(i, 2 * pair + 1).wait()

    def pass_on(i, arrival, buf, size, sends, recvs):
        for step in PAIR_ORDER:
            pair = (y_hi + step) % 4
            own_pair(arrival, i, pair)
            pl.when(has_next)(lambda: forward(buf, i, pair, size, sends, recvs).start())

    def previous(i, buf, size, sends, recvs):
        @pl.when(has_prev)
        def _():
            for pair in range(4):
                forward(buf, i, pair, size, sends, recvs).wait_recv()

        if i == K:
            @pl.when(jnp.logical_not(has_prev))
            def _():
                half = 8 * size
                buf[pl.ds(half, half), :] = buf[pl.ds(0, half), :]

    def spread(buf, left_buf, right_buf, size):
        half = 8 * size
        left = left_lanes((half, 128))
        one = jnp.ones((), BF16)
        own = buf[pl.ds(0, half), :]
        left_buf[pl.ds(0, half), :] = jnp.where(left, own, one)
        right_buf[pl.ds(0, half), :] = jnp.where(left, one, own)

    def spread_previous(buf, left_buf, right_buf, size):
        half = 8 * size
        left = left_lanes((half, 128))
        one = jnp.ones((), BF16)

        @pl.when(has_prev)
        def _():
            before = buf[pl.ds(half, half), :]
            left_buf[pl.ds(half, half), :] = jnp.where(left, before, one)
            right_buf[pl.ds(half, half), :] = jnp.where(left, one, before)

        @pl.when(jnp.logical_not(has_prev))
        def _():
            left_buf[pl.ds(half, half), :] = jnp.zeros((half, 128), BF16)
            right_buf[pl.ds(half, half), :] = jnp.zeros((half, 128), BF16)

    def weights(scores):
        return jnp.exp(scores - jnp.max(scores, axis=1, keepdims=True)).astype(BF16)

    scale = jnp.asarray(0.125, BF16)
    zero = jnp.zeros((), BF16)

    def o_tile(shard):
        return pltpu.make_async_remote_copy(
            src_ref=ot.at[rows_of(shard, ROWS)], dst_ref=ort.at[rows_of(y, ROWS)],
            send_sem=o_send_t.at[shard], recv_sem=o_recv_t.at[y],
            device_id=(frame, shard), device_id_type=MESH,
        )

    def o_head(shard):
        return pltpu.make_async_remote_copy(
            src_ref=oh.at[rows_of(shard, HALF)], dst_ref=orh.at[rows_of(y, HALF)],
            send_sem=o_send_h.at[shard], recv_sem=o_recv_h.at[y],
            device_id=(frame, shard), device_id_type=MESH,
        )

    def o_out(make, buf, back, size, recvs, pair):
        for shard in (2 * pair, 2 * pair + 1):
            own = owns & (space == shard)
            @pl.when(own)
            def _():
                pltpu.make_async_copy(buf.at[rows_of(shard, size)], back.at[rows_of(y, size)], recvs.at[y]).start()
            @pl.when(jnp.logical_not(own))
            def _():
                make(shard).start()

    def attend_tile(pair):
        own_pair(arrival_tile, Q, pair)
        q = qt[rows_of(pair, 2 * ROWS), :] * scale
        left = left_lanes(q.shape)
        a = jnp.dot(weights(dot_nt(jnp.where(left, q, zero), kt[...])), va[...], preferred_element_type=F32)
        b = jnp.dot(weights(dot_nt(jnp.where(left, zero, q), kt[...])), vb[...], preferred_element_type=F32)
        top = jnp.where(left, a, b)
        total = pltpu.roll(jnp.where(left, b, a), HALF, 1)
        ot[rows_of(pair, 2 * ROWS), :] = (top / total).astype(BF16)
        o_out(o_tile, ot, ort, ROWS, o_recv_t, pair)

    def attend_head(pair):
        own_pair(arrival_head, Q, pair)
        q = qh[rows_of(pair, 2 * HALF), :] * scale
        turned = swap_halves(q)
        left = left_lanes(q.shape)
        q_left = jnp.concatenate([jnp.where(left, q, zero), jnp.where(left, turned, zero)], 0)
        q_right = jnp.concatenate([jnp.where(left, zero, turned), jnp.where(left, zero, q)], 0)
        keys = kh[...]
        w = weights(jnp.concatenate([dot_nt(q_left, keys), dot_nt(q_right, keys)], 1))
        a = jnp.dot(w[:, :1024], ha[...], preferred_element_type=F32)
        b = jnp.dot(w[:, 1024:], hb[...], preferred_element_type=F32)
        both = a + pltpu.roll(b, HALF, 1)
        mixed = both / pltpu.roll(both, HALF, 1)
        oh[rows_of(pair, 2 * HALF), :] = jnp.where(
            left, mixed[:ROWS], pltpu.roll(mixed[ROWS:], HALF, 1)
        ).astype(BF16)
        o_out(o_head, oh, orh, HALF, o_recv_h, pair)

    def shifted(tile):
        return pltpu.make_async_remote_copy(
            src_ref=den_ref.at[0, :, columns(tile)], dst_ref=next_ref.at[0, :, columns(tile)],
            send_sem=shift_send.at[tile], recv_sem=shift_recv.at[tile],
            device_id=(queue - 1, space), device_id_type=MESH,
        )

    with jax.named_scope("wait_k"):
        pass_on(K, arrival_tile, kt, ROWS, fwd_send_t, fwd_recv_t)
    with jax.named_scope("wait_v"):
        pass_on(V, arrival_tile, vt, ROWS, fwd_send_t, fwd_recv_t)
    spread(vt, va, vb, ROWS)
    with jax.named_scope("wait_prev"):
        previous(K, kt, ROWS, fwd_send_t, fwd_recv_t)
        previous(V, vt, ROWS, fwd_send_t, fwd_recv_t)
    spread_previous(vt, va, vb, ROWS)
    for n, step in enumerate(PAIR_ORDER):
        with jax.named_scope("attend_tile"):
            attend_tile((y_hi + step) % 4)
        if n == 1:
            with jax.named_scope("wait_kh"):
                pass_on(K, arrival_head, kh, HALF, fwd_send_h, fwd_recv_h)
        if n == 2:
            with jax.named_scope("wait_vh"):
                pass_on(V, arrival_head, vh, HALF, fwd_send_h, fwd_recv_h)
    with jax.named_scope("wait_prev_h"):
        spread(vh, ha, hb, HALF)
        previous(K, kh, HALF, fwd_send_h, fwd_recv_h)
        previous(V, vh, HALF, fwd_send_h, fwd_recv_h)
        spread_previous(vh, ha, hb, HALF)

    gate_load.wait()
    step_now = plan_ref[levels_ref[0]]
    gate = gate_buf[pl.ds(step_now, 1), :]

    def gated(tile, attn):
        cut = slice(tile * 128, tile * 128 + 128)
        den_ref[0, :, cut] = (gate[:, cut] * attn.astype(F32)).astype(BF16)
        pl.when(has_ahead)(lambda: shifted(tile).start())

    def finish_tiles():
        for group in range(GROUPS):
            pltpu.make_async_copy(ort.at[pl.ds(0, ROWS)], ort.at[pl.ds(0, ROWS)], o_recv_t.at[group]).wait()
            gated(tile_of(group), ort[group * ROWS : (group + 1) * ROWS, :])

    def finish_heads():
        left = left_lanes((HALF, 128))
        for pair in range(4):
            for group in (2 * pair, 2 * pair + 1):
                pltpu.make_async_copy(orh.at[pl.ds(0, HALF)], orh.at[pl.ds(0, HALF)], o_recv_h.at[group]).wait()
            even = orh[2 * pair * HALF : (2 * pair + 1) * HALF, :]
            odd = orh[(2 * pair + 1) * HALF : (2 * pair + 2) * HALF, :]
            gated(
                3 * pair + 1,
                jnp.concatenate(
                    [jnp.where(left, even, swap_halves(odd)), jnp.where(left, swap_halves(even), odd)], 0
                ),
            )

    for n, step in enumerate(PAIR_ORDER):
        with jax.named_scope("attend_head"):
            attend_head((y_hi + step) % 4)
        if n == 2:
            with jax.named_scope("finish_tiles"):
                finish_tiles()
    with jax.named_scope("finish_heads"):
        finish_heads()

    @pl.when(jnp.logical_not(has_behind))
    def _():
        copy = pltpu.make_async_copy(fresh_hbm, next_ref.at[0], fresh_sem)
        copy.start()
        copy.wait()

    with jax.named_scope("wait_shift"):
        @pl.when(has_behind)
        def _():
            for tile in range(12):
                shifted(tile).wait_recv()

    with jax.named_scope("wait_sends"):
        @pl.when(has_ahead)
        def _():
            for tile in range(12):
                shifted(tile).wait_send()

        @pl.when(has_next)
        def _():
            for pair in range(4):
                for i, tiles, heads in ((K, kt, kh), (V, vt, vh)):
                    forward(tiles, i, pair, ROWS, fwd_send_t, fwd_recv_t).wait_send()
                    forward(heads, i, pair, HALF, fwd_send_h, fwd_recv_h).wait_send()

        for group in range(GROUPS):
            @pl.when(jnp.logical_not(owns & (group == y)))
            def _():
                for i in (K, V, Q):
                    sent_tile(i, group).wait_send()
                    sent_head(i, group).wait_send()

        for shard in range(8):
            @pl.when(jnp.logical_not(owns & (space == shard)))
            def _():
                o_tile(shard).wait_send()
                o_head(shard).wait_send()


def body(queries, keys, values, levels, plan, gate_table, fresh):
    vmem = functools.partial(pltpu.VMEM, dtype=BF16)
    dma = lambda *shape: pltpu.SemaphoreType.DMA(shape)
    any_space = pl.BlockSpec(memory_space=pl.ANY)
    smem = pl.BlockSpec(memory_space=pltpu.SMEM)
    out = jax.ShapeDtypeStruct((1, ROWS, COLS), BF16)
    return pl.pallas_call(
        kernel,
        out_shape=(out, out),
        in_specs=[any_space, any_space, any_space, smem, smem, any_space, any_space],
        out_specs=[pl.BlockSpec(memory_space=pltpu.VMEM)] * 2,
        scratch_shapes=[
            vmem((3, ROWS, COLS)), vmem((3, GROUPS, HALF, 128)), pltpu.VMEM((128, COLS), F32),
            vmem((2048, 128)), vmem((2048, 128)), vmem((1024, 128)),
            vmem((1024, 128)), vmem((1024, 128)), vmem((512, 128)),
            vmem((2048, 128)), vmem((2048, 128)), vmem((1024, 128)), vmem((1024, 128)),
            vmem((1024, 128)), vmem((512, 128)), vmem((1024, 128)), vmem((512, 128)),
            dma(3), pltpu.SemaphoreType.DMA,
            dma(3, 8), dma(3, 8), dma(3, 8), dma(3, 8),
            dma(2, 4), dma(2, 4), dma(2, 4), dma(2, 4),
            dma(8), dma(8), dma(8), dma(8),
            dma(12), dma(12), pltpu.SemaphoreType.DMA,
        ],
        compiler_params=pltpu.CompilerParams(
            collective_id=0, has_side_effects=True, vmem_limit_bytes=48 * 1024 * 1024
        ),
        name="frame_attention",
    )(queries, keys, values, levels, plan, gate_table, fresh)


def solution(mesh):
    return jax.shard_map(
        body,
        mesh=mesh,
        in_specs=(
            P("queue", "space", None),
            P("queue", "space", None),
            P("queue", "space", None),
            P("queue"),
            P(),
            P(),
            P("space", None),
        ),
        out_specs=(P("queue", "space", None), P("queue", "space", None)),
        check_vma=False,
    )
```

```python
import functools

import jax
import jax.numpy as jnp
from jax import lax
from jax.experimental import pallas as pl
from jax.experimental.pallas import tpu as pltpu
from jax.sharding import PartitionSpec as P

MESH = pl.DeviceIdType.MESH
BF16 = jnp.bfloat16
F32 = jnp.float32
ROWS = 128
HALF = 64
COLS = 1536
GROUPS = 8
NEAR_FIRST = (0, 1, 7, 2, 6, 3, 5, 4)
K, V, Q = 0, 1, 2


def dot_nt(a, b):
    return lax.dot_general(a, b, (((1,), (1,)), ((), ())), preferred_element_type=F32)


def left_lanes(shape):
    return lax.broadcasted_iota(jnp.int32, shape, len(shape) - 1) < HALF


def swap_halves(a):
    return pltpu.roll(a.astype(F32), HALF, a.ndim - 1).astype(a.dtype)


def tile_of(group):
    return 3 * (group // 2) + 2 * (group % 2)


def columns(tile):
    return pl.ds(pl.multiple_of(tile * 128, 128), 128)


def kernel(
    q_hbm, k_hbm, v_hbm, levels_ref, plan_ref, gate_hbm, fresh_hbm,
    den_ref, next_ref,
    src, packed, gate_buf, gate_row,
    kt, vt, qt, kh, vh, qh,
    va, vb, ha, hb,
    ot, oh, ort, orh,
    in_sem, gate_sem,
    send_t, recv_t, send_h, recv_h,
    fwd_send_t, fwd_recv_t, fwd_send_h, fwd_recv_h,
    o_send_t, o_recv_t, o_send_h, o_recv_h,
    shift_send, shift_recv, fresh_sem,
):
    queue = lax.axis_index("queue")
    space = lax.axis_index("space")
    z, y_lo, x = queue // 8, (queue // 4) % 2, queue % 4
    y_hi, core = space // 2, space % 2
    y = y_hi * 2 + y_lo
    frame = z * 8 + core * 4 + x
    nearer = 3 - 2 * y_lo
    near_pairs = [(y_hi + step) % 4 for step in (0, nearer, 4 - nearer, 2)]
    tokens_in = (kt, vt, qt)
    heads_in = (kh, vh, qh)

    def worker(of_frame, group):
        return (
            (of_frame // 8) * 8 + (group % 2) * 4 + of_frame % 4,
            (group // 2) * 2 + (of_frame // 4) % 2,
        )

    inputs = (k_hbm, v_hbm, q_hbm)
    loads = [
        pltpu.make_async_copy(ref.at[0], src.at[i], in_sem.at[i]) for i, ref in enumerate(inputs)
    ]
    gate_load = pltpu.make_async_copy(gate_hbm, gate_buf, gate_sem)

    barrier = pltpu.get_barrier_semaphore()

    def greet(device):
        pl.semaphore_signal(barrier, inc=1, device_id=device, device_id_type=MESH)

    has_prev, has_next = frame > 0, frame < 63
    has_ahead, has_behind = queue > 0, queue < 63
    owns = core == y_lo
    for i in range(8):
        @pl.when(jnp.logical_not(owns & (space == i)))
        def _():
            greet((frame, i))
    pl.when(has_prev)(lambda: greet(worker(frame - 1, y)))
    pl.when(has_behind)(lambda: greet((queue + 1, space)))
    for i in range(GROUPS):
        @pl.when(jnp.logical_not(owns & (y == i)))
        def _():
            greet(worker(queue, i))
    greeted = (
        16
        - 2 * owns.astype(jnp.int32)
        + has_next.astype(jnp.int32)
        + has_ahead.astype(jnp.int32)
    )

    def pack(i):
        left = left_lanes((HALF, 128))
        for pair in range(4):
            tile = src[i, :, (3 * pair + 1) * 128 : (3 * pair + 2) * 128]
            top, bottom = tile[:HALF], tile[HALF:]
            packed[i, 2 * pair] = jnp.where(left, top, swap_halves(bottom))
            packed[i, 2 * pair + 1] = jnp.where(left, swap_halves(top), bottom)

    for load in loads:
        load.start()
    gate_load.start()
    pl.semaphore_wait(barrier, greeted)

    def rows_of(index, size):
        return pl.ds(pl.multiple_of(index * size, size), size)

    def sent_tile(i, group):
        return pltpu.make_async_remote_copy(
            src_ref=src.at[i, :, columns(tile_of(group))],
            dst_ref=tokens_in[i].at[rows_of(space, ROWS)],
            send_sem=send_t.at[i, group], recv_sem=recv_t.at[i, space],
            device_id=worker(queue, group), device_id_type=MESH,
        )

    def sent_head(i, group):
        return pltpu.make_async_remote_copy(
            src_ref=packed.at[i, group],
            dst_ref=heads_in[i].at[rows_of(space, HALF)],
            send_sem=send_h.at[i, group], recv_sem=recv_h.at[i, space],
            device_id=worker(queue, group), device_id_type=MESH,
        )

    def send_out(make, kept, i):
        for shift in NEAR_FIRST:
            group = (y + shift) % GROUPS
            if shift:
                make(i, group).start()
            else:
                pl.when(owns)(lambda: kept(i).start())
                pl.when(jnp.logical_not(owns))(lambda: make(i, group).start())

    def kept_tile(i):
        return pltpu.make_async_copy(
            src.at[i, :, columns(tile_of(y))],
            tokens_in[i].at[rows_of(space, ROWS)],
            recv_t.at[i, space],
        )

    def kept_head(i):
        return pltpu.make_async_copy(
            packed.at[i, y],
            heads_in[i].at[rows_of(space, HALF)],
            recv_h.at[i, space],
        )

    with jax.named_scope("send_all"):
        for i in (K, V, Q):
            loads[i].wait()
            send_out(sent_tile, kept_tile, i)
            pack(i)
        for i in (K, V):
            send_out(sent_head, kept_head, i)

    def arrival_tile(i, shard):
        return pltpu.make_async_copy(
            tokens_in[i].at[rows_of(shard, ROWS)], tokens_in[i].at[rows_of(shard, ROWS)], recv_t.at[i, shard]
        )

    def arrival_head(i, shard):
        return pltpu.make_async_copy(
            heads_in[i].at[rows_of(shard, HALF)], heads_in[i].at[rows_of(shard, HALF)], recv_h.at[i, shard]
        )

    def forward(buf, i, pair, size, sends, recvs):
        return pltpu.make_async_remote_copy(
            src_ref=buf.at[rows_of(pair, 2 * size)],
            dst_ref=buf.at[rows_of(4 + pair, 2 * size)],
            send_sem=sends.at[i, pair], recv_sem=recvs.at[i, pair],
            device_id=worker(frame + 1, y), device_id_type=MESH,
        )

    def own_pair(arrival, i, pair):
        arrival(i, 2 * pair).wait()
        arrival(i, 2 * pair + 1).wait()

    def pass_on(i, arrival, buf, size, sends, recvs):
        for pair in near_pairs:
            own_pair(arrival, i, pair)
            pl.when(has_next)(lambda: forward(buf, i, pair, size, sends, recvs).start())

    def previous(i, buf, size, sends, recvs):
        @pl.when(has_prev)
        def _():
            for pair in range(4):
                forward(buf, i, pair, size, sends, recvs).wait_recv()

        if i == K:
            @pl.when(jnp.logical_not(has_prev))
            def _():
                half = 8 * size
                buf[pl.ds(half, half), :] = buf[pl.ds(0, half), :]

    def spread(buf, left_buf, right_buf, size):
        half = 8 * size
        left = left_lanes((half, 128))
        one = jnp.ones((), BF16)
        own = buf[pl.ds(0, half), :]
        left_buf[pl.ds(0, half), :] = jnp.where(left, own, one)
        right_buf[pl.ds(0, half), :] = jnp.where(left, one, own)

    def spread_previous(buf, left_buf, right_buf, size):
        half = 8 * size
        left = left_lanes((half, 128))
        one = jnp.ones((), BF16)

        @pl.when(has_prev)
        def _():
            before = buf[pl.ds(half, half), :]
            left_buf[pl.ds(half, half), :] = jnp.where(left, before, one)
            right_buf[pl.ds(half, half), :] = jnp.where(left, one, before)

        @pl.when(jnp.logical_not(has_prev))
        def _():
            left_buf[pl.ds(half, half), :] = jnp.zeros((half, 128), BF16)
            right_buf[pl.ds(half, half), :] = jnp.zeros((half, 128), BF16)

    def weights(scores):
        return jnp.exp(scores - jnp.max(scores, axis=1, keepdims=True)).astype(BF16)

    scale = jnp.asarray(0.125, BF16)
    zero = jnp.zeros((), BF16)

    def o_tile(shard):
        return pltpu.make_async_remote_copy(
            src_ref=ot.at[rows_of(shard, ROWS)], dst_ref=ort.at[rows_of(y, ROWS)],
            send_sem=o_send_t.at[shard], recv_sem=o_recv_t.at[y],
            device_id=(frame, shard), device_id_type=MESH,
        )

    def o_head(shard):
        return pltpu.make_async_remote_copy(
            src_ref=oh.at[rows_of(shard, HALF)], dst_ref=orh.at[rows_of(y, HALF)],
            send_sem=o_send_h.at[shard], recv_sem=o_recv_h.at[y],
            device_id=(frame, shard), device_id_type=MESH,
        )

    def o_out(make, buf, back, size, recvs, pair):
        for shard in (2 * pair, 2 * pair + 1):
            own = owns & (space == shard)
            @pl.when(own)
            def _():
                pltpu.make_async_copy(buf.at[rows_of(shard, size)], back.at[rows_of(y, size)], recvs.at[y]).start()
            @pl.when(jnp.logical_not(own))
            def _():
                make(shard).start()

    def attend_tile(pair):
        own_pair(arrival_tile, Q, pair)
        q = qt[rows_of(pair, 2 * ROWS), :] * scale
        left = left_lanes(q.shape)
        a = jnp.dot(weights(dot_nt(jnp.where(left, q, zero), kt[...])), va[...], preferred_element_type=F32)
        b = jnp.dot(weights(dot_nt(jnp.where(left, zero, q), kt[...])), vb[...], preferred_element_type=F32)
        top = jnp.where(left, a, b)
        total = pltpu.roll(jnp.where(left, b, a), HALF, 1)
        ot[rows_of(pair, 2 * ROWS), :] = (top / total).astype(BF16)
        o_out(o_tile, ot, ort, ROWS, o_recv_t, pair)

    def attend_head(pair):
        own_pair(arrival_head, Q, pair)
        q = qh[rows_of(pair, 2 * HALF), :] * scale
        turned = swap_halves(q)
        left = left_lanes(q.shape)
        q_left = jnp.concatenate([jnp.where(left, q, zero), jnp.where(left, turned, zero)], 0)
        q_right = jnp.concatenate([jnp.where(left, zero, turned), jnp.where(left, zero, q)], 0)
        keys = kh[...]
        w = weights(jnp.concatenate([dot_nt(q_left, keys), dot_nt(q_right, keys)], 1))
        a = jnp.dot(w[:, :1024], ha[...], preferred_element_type=F32)
        b = jnp.dot(w[:, 1024:], hb[...], preferred_element_type=F32)
        both = a + pltpu.roll(b, HALF, 1)
        mixed = both / pltpu.roll(both, HALF, 1)
        oh[rows_of(pair, 2 * HALF), :] = jnp.where(
            left, mixed[:ROWS], pltpu.roll(mixed[ROWS:], HALF, 1)
        ).astype(BF16)
        o_out(o_head, oh, orh, HALF, o_recv_h, pair)

    def shifted(tile):
        return pltpu.make_async_remote_copy(
            src_ref=den_ref.at[0, :, columns(tile)], dst_ref=next_ref.at[0, :, columns(tile)],
            send_sem=shift_send.at[tile], recv_sem=shift_recv.at[tile],
            device_id=(queue - 1, space), device_id_type=MESH,
        )

    with jax.named_scope("wait_k"):
        pass_on(K, arrival_tile, kt, ROWS, fwd_send_t, fwd_recv_t)
    with jax.named_scope("wait_v"):
        pass_on(V, arrival_tile, vt, ROWS, fwd_send_t, fwd_recv_t)
    spread(vt, va, vb, ROWS)
    with jax.named_scope("wait_prev"):
        previous(K, kt, ROWS, fwd_send_t, fwd_recv_t)
        previous(V, vt, ROWS, fwd_send_t, fwd_recv_t)
    spread_previous(vt, va, vb, ROWS)
    for n, pair in enumerate(near_pairs):
        with jax.named_scope("attend_tile"):
            attend_tile(pair)
        if n == 1:
            send_out(sent_head, kept_head, Q)
        if n == 1:
            with jax.named_scope("wait_kh"):
                pass_on(K, arrival_head, kh, HALF, fwd_send_h, fwd_recv_h)
        if n == 2:
            with jax.named_scope("wait_vh"):
                pass_on(V, arrival_head, vh, HALF, fwd_send_h, fwd_recv_h)

    gate_load.wait()
    step_now = plan_ref[levels_ref[0]]
    gate_row[...] = gate_buf[pl.ds(step_now, 1), :]

    def gated(tile, attn):
        cut = columns(tile)
        den_ref[0, :, cut] = (gate_row[:, cut] * attn.astype(F32)).astype(BF16)
        pl.when(has_ahead)(lambda: shifted(tile).start())

    def arrived(back, index, size, recvs):
        pltpu.make_async_copy(
            back.at[rows_of(index, size)], back.at[rows_of(index, size)], recvs.at[index]
        ).wait()

    def finish_tile(group):
        arrived(ort, group, ROWS, o_recv_t)
        gated(tile_of(group), ort[rows_of(group, ROWS), :])

    def finish_heads(pair):
        left = left_lanes((HALF, 128))
        for group in (2 * pair, 2 * pair + 1):
            arrived(orh, group, HALF, o_recv_h)
        even = orh[rows_of(2 * pair, HALF), :]
        odd = orh[rows_of(2 * pair + 1, HALF), :]
        gated(
            3 * pair + 1,
            jnp.concatenate(
                [jnp.where(left, even, swap_halves(odd)), jnp.where(left, swap_halves(even), odd)], 0
            ),
        )

    with jax.named_scope("wait_prev_h"):
        spread(vh, ha, hb, HALF)
        previous(K, kh, HALF, fwd_send_h, fwd_recv_h)
        previous(V, vh, HALF, fwd_send_h, fwd_recv_h)
        spread_previous(vh, ha, hb, HALF)

    home = [(y_hi + step) % 4 for step in (0, 1, 3, 2)]
    tile_groups = [2 * home[0], 2 * home[0] + 1, 2 * home[1], 2 * home[2] + 1,
                   2 * home[2], 2 * home[1] + 1, 2 * home[3], 2 * home[3] + 1]
    for group in tile_groups[:4]:
        finish_tile(group)
    for n, pair in enumerate(near_pairs):
        with jax.named_scope("attend_head"):
            attend_head(pair)
    with jax.named_scope("finish"):
        for group in tile_groups[4:]:
            finish_tile(group)
        for pair in home:
            finish_heads(pair)
    @pl.when(jnp.logical_not(has_behind))
    def _():
        copy = pltpu.make_async_copy(fresh_hbm, next_ref.at[0], fresh_sem)
        copy.start()
        copy.wait()

    with jax.named_scope("wait_shift"):
        @pl.when(has_behind)
        def _():
            for tile in range(12):
                shifted(tile).wait_recv()

    with jax.named_scope("wait_sends"):
        @pl.when(has_ahead)
        def _():
            for tile in range(12):
                shifted(tile).wait_send()

        @pl.when(has_next)
        def _():
            for pair in range(4):
                for i, tiles, heads in ((K, kt, kh), (V, vt, vh)):
                    forward(tiles, i, pair, ROWS, fwd_send_t, fwd_recv_t).wait_send()
                    forward(heads, i, pair, HALF, fwd_send_h, fwd_recv_h).wait_send()

        for group in range(GROUPS):
            @pl.when(jnp.logical_not(owns & (group == y)))
            def _():
                for i in (K, V, Q):
                    sent_tile(i, group).wait_send()
                    sent_head(i, group).wait_send()

        for shard in range(8):
            @pl.when(jnp.logical_not(owns & (space == shard)))
            def _():
                o_tile(shard).wait_send()
                o_head(shard).wait_send()


def hand_over(den_ref, next_ref, den_out, next_out, sems):
    copies = [
        pltpu.make_async_copy(den_ref, den_out, sems.at[0]),
        pltpu.make_async_copy(next_ref, next_out, sems.at[1]),
    ]
    for copy in copies:
        copy.start()
    for copy in copies:
        copy.wait()


def body(queries, keys, values, levels, plan, gate_table, fresh):
    vmem = functools.partial(pltpu.VMEM, dtype=BF16)
    dma = lambda *shape: pltpu.SemaphoreType.DMA(shape)
    any_space = pl.BlockSpec(memory_space=pl.ANY)
    smem = pl.BlockSpec(memory_space=pltpu.SMEM)
    out = jax.ShapeDtypeStruct((1, ROWS, COLS), BF16)
    results = pl.pallas_call(
        kernel,
        out_shape=(out, out),
        in_specs=[any_space, any_space, any_space, smem, smem, any_space, any_space],
        out_specs=[pl.BlockSpec(memory_space=pltpu.VMEM)] * 2,
        scratch_shapes=[
            vmem((3, ROWS, COLS)), vmem((3, GROUPS, HALF, 128)), pltpu.VMEM((128, COLS), F32), pltpu.VMEM((1, COLS), F32),
            vmem((2048, 128)), vmem((2048, 128)), vmem((1024, 128)),
            vmem((1024, 128)), vmem((1024, 128)), vmem((512, 128)),
            vmem((2048, 128)), vmem((2048, 128)), vmem((1024, 128)), vmem((1024, 128)),
            vmem((1024, 128)), vmem((512, 128)), vmem((1024, 128)), vmem((512, 128)),
            dma(3), pltpu.SemaphoreType.DMA,
            dma(3, 8), dma(3, 8), dma(3, 8), dma(3, 8),
            dma(2, 4), dma(2, 4), dma(2, 4), dma(2, 4),
            dma(8), dma(8), dma(8), dma(8),
            dma(12), dma(12), pltpu.SemaphoreType.DMA,
        ],
        compiler_params=pltpu.CompilerParams(
            collective_id=0, has_side_effects=True, vmem_limit_bytes=53 * 1024 * 1024
        ),
        name="frame_attention",
    )(queries, keys, values, levels, plan, gate_table, fresh)
    return pl.pallas_call(
        hand_over,
        out_shape=(out, out),
        in_specs=[pl.BlockSpec(memory_space=pl.ANY)] * 2,
        out_specs=[pl.BlockSpec(memory_space=pl.ANY)] * 2,
        scratch_shapes=[dma(2)],
        compiler_params=pltpu.CompilerParams(vmem_limit_bytes=8 * 1024 * 1024),
        name="hand_over",
    )(*results)


def solution(mesh):
    return jax.shard_map(
        body,
        mesh=mesh,
        in_specs=(
            P("queue", "space", None),
            P("queue", "space", None),
            P("queue", "space", None),
            P("queue"),
            P(),
            P(),
            P("space", None),
        ),
        out_specs=(P("queue", "space", None), P("queue", "space", None)),
        check_vma=False,
    )
```

```python
import functools

import jax
import jax.numpy as jnp
from jax import lax
from jax.experimental import pallas as pl
from jax.experimental.pallas import tpu as pltpu
from jax.sharding import PartitionSpec as P

MESH = pl.DeviceIdType.MESH
BF16 = jnp.bfloat16
F32 = jnp.float32
ROWS = 128
HALF = 64
COLS = 1536
GROUPS = 8
NEAR_FIRST = (0, 1, 7, 2, 6, 3, 5, 4)
K, V, Q = 0, 1, 2
VIA = (3, 1, 2, 3)


def dot_nt(a, b):
    return lax.dot_general(a, b, (((1,), (1,)), ((), ())), preferred_element_type=F32)


def left_lanes(shape):
    return lax.broadcasted_iota(jnp.int32, shape, len(shape) - 1) < HALF


def swap_halves(a):
    return pltpu.roll(a.astype(F32), HALF, a.ndim - 1).astype(a.dtype)


def tile_of(group):
    return 3 * (group // 2) + 2 * (group % 2)


def columns(tile):
    return pl.ds(pl.multiple_of(tile * 128, 128), 128)


def kernel(
    q_hbm, k_hbm, v_hbm, levels_hbm, plan_hbm, gate_hbm, fresh_hbm,
    den_ref, next_ref,
    levels_ref, plan_ref, index_sem,
    src, packed, gate_buf, gate_row,
    kt, vt, qt, kh, vh, qh,
    va, vb, ha, hb,
    ot, oh, ort, orh,
    in_sem, gate_sem,
    send_t, recv_t, send_h, recv_h,
    fwd_send_t, fwd_recv_t, fwd_send_h, fwd_recv_h,
    o_send_t, o_recv_t, o_send_h, o_recv_h,
    shift_send, shift_recv, fresh_sem,
    relay_buf, relay_send, relay_recv,
):
    queue = lax.axis_index("queue")
    space = lax.axis_index("space")
    z, y_lo, x = queue // 8, (queue // 4) % 2, queue % 4
    y_hi, core = space // 2, space % 2
    y = y_hi * 2 + y_lo
    frame = z * 8 + core * 4 + x
    nearer = 3 - 2 * y_lo
    near_pairs = [(y_hi + step) % 4 for step in (0, nearer, 4 - nearer, 2)]
    tokens_in = (kt, vt, qt)
    heads_in = (kh, vh, qh)

    def worker(of_frame, group):
        return (
            (of_frame // 8) * 8 + (group % 2) * 4 + of_frame % 4,
            (group // 2) * 2 + (of_frame // 4) % 2,
        )

    inputs = (k_hbm, v_hbm, q_hbm)
    loads = [
        pltpu.make_async_copy(ref.at[0], src.at[i], in_sem.at[i]) for i, ref in enumerate(inputs)
    ]
    gate_load = pltpu.make_async_copy(gate_hbm, gate_buf, gate_sem)

    for load in loads:
        load.start()
    gate_load.start()
    index_loads = [
        pltpu.make_async_copy(levels_hbm, levels_ref, index_sem.at[0]),
        pltpu.make_async_copy(plan_hbm, plan_ref, index_sem.at[1]),
    ]
    for load in index_loads:
        load.start()

    barrier = pltpu.get_barrier_semaphore()

    def greet(device):
        pl.semaphore_signal(barrier, inc=1, device_id=device, device_id_type=MESH)

    has_prev, has_next = frame > 0, frame < 63
    has_ahead, has_behind = queue > 0, queue < 63
    wraps = has_ahead & (x == 0)
    relays = (x > 0) & (queue - x > 0)
    owns = core == y_lo
    for i in range(8):
        @pl.when(jnp.logical_not(owns & (space == i)))
        def _():
            greet((frame, i))
    pl.when(has_prev)(lambda: greet(worker(frame - 1, y)))
    pl.when(has_behind)(lambda: greet((queue + 1, space)))

    @pl.when(has_behind & (x == 3))
    def _():
        for column in sorted(set(VIA)):
            greet((queue + 1 + column, space))

    for column in sorted(set(VIA)):
        pl.when(relays & (x == column))(lambda: greet((queue - x, space)))
    for i in range(GROUPS):
        @pl.when(jnp.logical_not(owns & (y == i)))
        def _():
            greet(worker(queue, i))
    greeted = (
        16
        - 2 * owns.astype(jnp.int32)
        + has_next.astype(jnp.int32)
        + has_ahead.astype(jnp.int32)
        + len(set(VIA)) * wraps.astype(jnp.int32)
        + sum((relays & (x == column)).astype(jnp.int32) for column in sorted(set(VIA)))
    )

    def pack(i):
        left = left_lanes((HALF, 128))
        for pair in range(4):
            tile = src[i, :, (3 * pair + 1) * 128 : (3 * pair + 2) * 128]
            top, bottom = tile[:HALF], tile[HALF:]
            packed[i, 2 * pair] = jnp.where(left, top, swap_halves(bottom))
            packed[i, 2 * pair + 1] = jnp.where(left, swap_halves(top), bottom)

    pl.semaphore_wait(barrier, greeted)

    def rows_of(index, size):
        return pl.ds(pl.multiple_of(index * size, size), size)

    def sent_tile(i, group):
        return pltpu.make_async_remote_copy(
            src_ref=src.at[i, :, columns(tile_of(group))],
            dst_ref=tokens_in[i].at[rows_of(space, ROWS)],
            send_sem=send_t.at[i, group], recv_sem=recv_t.at[i, space],
            device_id=worker(queue, group), device_id_type=MESH,
        )

    def sent_head(i, group):
        return pltpu.make_async_remote_copy(
            src_ref=packed.at[i, group],
            dst_ref=heads_in[i].at[rows_of(space, HALF)],
            send_sem=send_h.at[i, group], recv_sem=recv_h.at[i, space],
            device_id=worker(queue, group), device_id_type=MESH,
        )

    def send_out(make, kept, i, order=NEAR_FIRST):
        for shift in order:
            group = (y + shift) % GROUPS
            if shift:
                make(i, group).start()
            else:
                pl.when(owns)(lambda: kept(i).start())
                pl.when(jnp.logical_not(owns))(lambda: make(i, group).start())

    def kept_tile(i):
        return pltpu.make_async_copy(
            src.at[i, :, columns(tile_of(y))],
            tokens_in[i].at[rows_of(space, ROWS)],
            recv_t.at[i, space],
        )

    def kept_head(i):
        return pltpu.make_async_copy(
            packed.at[i, y],
            heads_in[i].at[rows_of(space, HALF)],
            recv_h.at[i, space],
        )

    with jax.named_scope("send_all"):
        for i in (K, V, Q):
            loads[i].wait()
            send_out(sent_tile, kept_tile, i)
            pack(i)
        for i in (K, V):
            send_out(sent_head, kept_head, i)

    def arrival_tile(i, shard):
        return pltpu.make_async_copy(
            tokens_in[i].at[rows_of(shard, ROWS)], tokens_in[i].at[rows_of(shard, ROWS)], recv_t.at[i, shard]
        )

    def arrival_head(i, shard):
        return pltpu.make_async_copy(
            heads_in[i].at[rows_of(shard, HALF)], heads_in[i].at[rows_of(shard, HALF)], recv_h.at[i, shard]
        )

    def forward(buf, i, pair, size, sends, recvs):
        return pltpu.make_async_remote_copy(
            src_ref=buf.at[rows_of(pair, 2 * size)],
            dst_ref=buf.at[rows_of(4 + pair, 2 * size)],
            send_sem=sends.at[i, pair], recv_sem=recvs.at[i, pair],
            device_id=worker(frame + 1, y), device_id_type=MESH,
        )

    def own_pair(arrival, i, pair):
        arrival(i, 2 * pair).wait()
        arrival(i, 2 * pair + 1).wait()

    def pass_on(i, arrival, buf, size, sends, recvs):
        for pair in near_pairs:
            own_pair(arrival, i, pair)
            pl.when(has_next)(lambda: forward(buf, i, pair, size, sends, recvs).start())

    def previous(i, buf, size, sends, recvs):
        @pl.when(has_prev)
        def _():
            for pair in range(4):
                forward(buf, i, pair, size, sends, recvs).wait_recv()

        if i == K:
            @pl.when(jnp.logical_not(has_prev))
            def _():
                half = 8 * size
                buf[pl.ds(half, half), :] = buf[pl.ds(0, half), :]

    def spread(buf, left_buf, right_buf, size):
        half = 8 * size
        left = left_lanes((half, 128))
        one = jnp.ones((), BF16)
        own = buf[pl.ds(0, half), :]
        left_buf[pl.ds(0, half), :] = jnp.where(left, own, one)
        right_buf[pl.ds(0, half), :] = jnp.where(left, one, own)

    def spread_previous(buf, left_buf, right_buf, size):
        half = 8 * size
        left = left_lanes((half, 128))
        one = jnp.ones((), BF16)

        @pl.when(has_prev)
        def _():
            before = buf[pl.ds(half, half), :]
            left_buf[pl.ds(half, half), :] = jnp.where(left, before, one)
            right_buf[pl.ds(half, half), :] = jnp.where(left, one, before)

        @pl.when(jnp.logical_not(has_prev))
        def _():
            left_buf[pl.ds(half, half), :] = jnp.zeros((half, 128), BF16)
            right_buf[pl.ds(half, half), :] = jnp.zeros((half, 128), BF16)

    def weights(scores):
        return jnp.exp(scores - jnp.max(scores, axis=1, keepdims=True)).astype(BF16)

    scale = jnp.asarray(0.125, BF16)
    zero = jnp.zeros((), BF16)

    def o_tile(shard):
        return pltpu.make_async_remote_copy(
            src_ref=ot.at[rows_of(shard, ROWS)], dst_ref=ort.at[rows_of(y, ROWS)],
            send_sem=o_send_t.at[shard], recv_sem=o_recv_t.at[y],
            device_id=(frame, shard), device_id_type=MESH,
        )

    def o_head(shard):
        return pltpu.make_async_remote_copy(
            src_ref=oh.at[rows_of(shard, HALF)], dst_ref=orh.at[rows_of(y, HALF)],
            send_sem=o_send_h.at[shard], recv_sem=o_recv_h.at[y],
            device_id=(frame, shard), device_id_type=MESH,
        )

    def o_out(make, buf, back, size, recvs, pair):
        for shard in (2 * pair, 2 * pair + 1):
            own = owns & (space == shard)
            @pl.when(own)
            def _():
                pltpu.make_async_copy(buf.at[rows_of(shard, size)], back.at[rows_of(y, size)], recvs.at[y]).start()
            @pl.when(jnp.logical_not(own))
            def _():
                make(shard).start()

    def attend_tile(pair):
        own_pair(arrival_tile, Q, pair)
        q = qt[rows_of(pair, 2 * ROWS), :] * scale
        left = left_lanes(q.shape)
        a = jnp.dot(weights(dot_nt(jnp.where(left, q, zero), kt[...])), va[...], preferred_element_type=F32)
        b = jnp.dot(weights(dot_nt(jnp.where(left, zero, q), kt[...])), vb[...], preferred_element_type=F32)
        top = jnp.where(left, a, b)
        total = pltpu.roll(jnp.where(left, b, a), HALF, 1)
        ot[rows_of(pair, 2 * ROWS), :] = (top / total).astype(BF16)
        o_out(o_tile, ot, ort, ROWS, o_recv_t, pair)

    def attend_head(pair):
        own_pair(arrival_head, Q, pair)
        q = qh[rows_of(pair, 2 * HALF), :] * scale
        turned = swap_halves(q)
        left = left_lanes(q.shape)
        q_left = jnp.concatenate([jnp.where(left, q, zero), jnp.where(left, turned, zero)], 0)
        q_right = jnp.concatenate([jnp.where(left, zero, turned), jnp.where(left, zero, q)], 0)
        keys = kh[...]
        w = weights(jnp.concatenate([dot_nt(q_left, keys), dot_nt(q_right, keys)], 1))
        a = jnp.dot(w[:, :1024], ha[...], preferred_element_type=F32)
        b = jnp.dot(w[:, 1024:], hb[...], preferred_element_type=F32)
        both = a + pltpu.roll(b, HALF, 1)
        mixed = both / pltpu.roll(both, HALF, 1)
        oh[rows_of(pair, 2 * HALF), :] = jnp.where(
            left, mixed[:ROWS], pltpu.roll(mixed[ROWS:], HALF, 1)
        ).astype(BF16)
        o_out(o_head, oh, orh, HALF, o_recv_h, pair)

    def shifted(tile):
        return pltpu.make_async_remote_copy(
            src_ref=den_ref.at[0, :, columns(tile)], dst_ref=next_ref.at[0, :, columns(tile)],
            send_sem=shift_send.at[tile], recv_sem=shift_recv.at[tile],
            device_id=(queue - 1, space), device_id_type=MESH,
        )

    def to_relay(tile, k):
        return pltpu.make_async_remote_copy(
            src_ref=den_ref.at[0, :, columns(tile)], dst_ref=relay_buf.at[k],
            send_sem=shift_send.at[tile], recv_sem=relay_recv.at[k],
            device_id=(queue + VIA[k], space), device_id_type=MESH,
        )

    def from_relay(tile, k):
        return pltpu.make_async_remote_copy(
            src_ref=relay_buf.at[k], dst_ref=next_ref.at[0, :, columns(tile)],
            send_sem=relay_send.at[k], recv_sem=shift_recv.at[tile],
            device_id=(queue - x - 1, space), device_id_type=MESH,
        )

    with jax.named_scope("wait_k"):
        pass_on(K, arrival_tile, kt, ROWS, fwd_send_t, fwd_recv_t)
    with jax.named_scope("wait_v"):
        pass_on(V, arrival_tile, vt, ROWS, fwd_send_t, fwd_recv_t)
    spread(vt, va, vb, ROWS)
    with jax.named_scope("wait_prev"):
        previous(K, kt, ROWS, fwd_send_t, fwd_recv_t)
        previous(V, vt, ROWS, fwd_send_t, fwd_recv_t)
    spread_previous(vt, va, vb, ROWS)
    for n, pair in enumerate(near_pairs):
        with jax.named_scope("attend_tile"):
            attend_tile(pair)
        if n == 0:
            send_out(sent_head, kept_head, Q, NEAR_FIRST[::-1])
        if n == 1:
            with jax.named_scope("wait_kh"):
                pass_on(K, arrival_head, kh, HALF, fwd_send_h, fwd_recv_h)
        if n == 2:
            with jax.named_scope("wait_vh"):
                pass_on(V, arrival_head, vh, HALF, fwd_send_h, fwd_recv_h)

    gate_load.wait()
    for load in index_loads:
        load.wait()
    step_now = plan_ref[levels_ref[0]]
    gate_row[...] = gate_buf[pl.ds(step_now, 1), :]

    def gated(tile, attn, k=len(VIA)):
        cut = columns(tile)
        den_ref[0, :, cut] = (gate_row[:, cut] * attn.astype(F32)).astype(BF16)
        if k < len(VIA):
            pl.when(has_ahead & (x > 0))(lambda: shifted(tile).start())
            pl.when(wraps)(lambda: to_relay(tile, k).start())
        else:
            pl.when(has_ahead)(lambda: shifted(tile).start())

    def arrived(back, index, size, recvs):
        pltpu.make_async_copy(
            back.at[rows_of(index, size)], back.at[rows_of(index, size)], recvs.at[index]
        ).wait()

    def finish_tile(k):
        group = tile_groups[k]
        arrived(ort, group, ROWS, o_recv_t)
        gated(tile_of(group), ort[rows_of(group, ROWS), :], k)

    def relay(act):
        for column in sorted(set(VIA)):
            @pl.when(relays & (x == column))
            def _():
                for k in range(len(VIA)):
                    if VIA[k] == column:
                        act(k)

    def pass_relayed(k):
        pltpu.make_async_copy(relay_buf.at[k], relay_buf.at[k], relay_recv.at[k]).wait()
        from_relay(tile_of(tile_groups[k]), k).start()

    def wait_relayed(k):
        from_relay(tile_of(tile_groups[k]), k).wait_send()

    def finish_heads(pair):
        left = left_lanes((HALF, 128))
        for group in (2 * pair, 2 * pair + 1):
            arrived(orh, group, HALF, o_recv_h)
        even = orh[rows_of(2 * pair, HALF), :]
        odd = orh[rows_of(2 * pair + 1, HALF), :]
        gated(
            3 * pair + 1,
            jnp.concatenate(
                [jnp.where(left, even, swap_halves(odd)), jnp.where(left, swap_halves(even), odd)], 0
            ),
        )

    with jax.named_scope("wait_prev_h"):
        spread(vh, ha, hb, HALF)
        previous(K, kh, HALF, fwd_send_h, fwd_recv_h)
        previous(V, vh, HALF, fwd_send_h, fwd_recv_h)
        spread_previous(vh, ha, hb, HALF)

    home = [(y_hi + step) % 4 for step in (0, 1, 3, 2)]
    tile_groups = [2 * home[0], 2 * home[0] + 1, 2 * home[1], 2 * home[2] + 1,
                   2 * home[2], 2 * home[1] + 1, 2 * home[3], 2 * home[3] + 1]
    for k in range(4):
        finish_tile(k)
    for pair in near_pairs[::-1]:
        with jax.named_scope("attend_head"):
            attend_head(pair)
    with jax.named_scope("sent"):
        @pl.when(has_next)
        def _():
            for pair in range(4):
                for i, tiles, heads in ((K, kt, kh), (V, vt, vh)):
                    forward(tiles, i, pair, ROWS, fwd_send_t, fwd_recv_t).wait_send()
                    forward(heads, i, pair, HALF, fwd_send_h, fwd_recv_h).wait_send()

        for group in range(GROUPS):
            @pl.when(jnp.logical_not(owns & (group == y)))
            def _():
                for i in (K, V, Q):
                    sent_tile(i, group).wait_send()
                    sent_head(i, group).wait_send()
    with jax.named_scope("finish"):
        relay(pass_relayed)
        for k in range(4, 8):
            finish_tile(k)
        for shard in range(8):
            @pl.when(jnp.logical_not(owns & (space == shard)))
            def _():
                o_tile(shard).wait_send()
        for pair in home[::-1]:
            finish_heads(pair)
    @pl.when(jnp.logical_not(has_behind))
    def _():
        copy = pltpu.make_async_copy(fresh_hbm, next_ref.at[0], fresh_sem)
        copy.start()
        copy.wait()

    with jax.named_scope("wait_shift"):
        @pl.when(has_behind)
        def _():
            for tile in range(12):
                shifted(tile).wait_recv()

    with jax.named_scope("wait_sends"):
        relay(wait_relayed)

        @pl.when(has_ahead)
        def _():
            for tile in range(12):
                shifted(tile).wait_send()

        for shard in range(8):
            @pl.when(jnp.logical_not(owns & (space == shard)))
            def _():
                o_head(shard).wait_send()


def hand_over(den_ref, next_ref, den_out, next_out, sems):
    copies = [
        pltpu.make_async_copy(den_ref, den_out, sems.at[0]),
        pltpu.make_async_copy(next_ref, next_out, sems.at[1]),
    ]
    for copy in copies:
        copy.start()
    for copy in copies:
        copy.wait()


def body(queries, keys, values, levels, plan, gate_table, fresh):
    vmem = functools.partial(pltpu.VMEM, dtype=BF16)
    dma = lambda *shape: pltpu.SemaphoreType.DMA(shape)
    any_space = pl.BlockSpec(memory_space=pl.ANY)
    out = jax.ShapeDtypeStruct((1, ROWS, COLS), BF16)
    results = pl.pallas_call(
        kernel,
        out_shape=(out, out),
        in_specs=[any_space] * 7,
        out_specs=[pl.BlockSpec(memory_space=pltpu.VMEM)] * 2,
        scratch_shapes=[
            pltpu.SMEM((1,), jnp.int32), pltpu.SMEM((64,), jnp.int32), dma(2),
            vmem((3, ROWS, COLS)), vmem((3, GROUPS, HALF, 128)), pltpu.VMEM((128, COLS), F32), pltpu.VMEM((1, COLS), F32),
            vmem((2048, 128)), vmem((2048, 128)), vmem((1024, 128)),
            vmem((1024, 128)), vmem((1024, 128)), vmem((512, 128)),
            vmem((2048, 128)), vmem((2048, 128)), vmem((1024, 128)), vmem((1024, 128)),
            vmem((1024, 128)), vmem((512, 128)), vmem((1024, 128)), vmem((512, 128)),
            dma(3), pltpu.SemaphoreType.DMA,
            dma(3, 8), dma(3, 8), dma(3, 8), dma(3, 8),
            dma(2, 4), dma(2, 4), dma(2, 4), dma(2, 4),
            dma(8), dma(8), dma(8), dma(8),
            dma(12), dma(12), pltpu.SemaphoreType.DMA,
            vmem((len(VIA), ROWS, 128)), dma(len(VIA)), dma(len(VIA)),
        ],
        compiler_params=pltpu.CompilerParams(
            collective_id=0, has_side_effects=True, vmem_limit_bytes=53 * 1024 * 1024
        ),
        name="frame_attention",
    )(queries, keys, values, levels, plan, gate_table, fresh)
    return pl.pallas_call(
        hand_over,
        out_shape=(out, out),
        in_specs=[pl.BlockSpec(memory_space=pl.ANY)] * 2,
        out_specs=[pl.BlockSpec(memory_space=pl.ANY)] * 2,
        scratch_shapes=[dma(2)],
        compiler_params=pltpu.CompilerParams(vmem_limit_bytes=8 * 1024 * 1024),
        name="hand_over",
    )(*results)


def solution(mesh):
    return jax.shard_map(
        body,
        mesh=mesh,
        in_specs=(
            P("queue", "space", None),
            P("queue", "space", None),
            P("queue", "space", None),
            P("queue"),
            P(),
            P(),
            P("space", None),
        ),
        out_specs=(P("queue", "space", None), P("queue", "space", None)),
        check_vma=False,
    )
```

```python
import functools

import jax
import jax.numpy as jnp
from jax import lax
from jax.experimental import pallas as pl
from jax.experimental.pallas import tpu as pltpu
from jax.sharding import PartitionSpec as P

MESH = pl.DeviceIdType.MESH
BF16 = jnp.bfloat16
F32 = jnp.float32
ROWS = 128
HALF = 64
COLS = 1536
GROUPS = 8
NEAR_FIRST = (0, 1, 7, 2, 6, 3, 5, 4)
K, V, Q = 0, 1, 2
VIA = (3, 1, 2, 3)


def dot_nt(a, b):
    return lax.dot_general(a, b, (((1,), (1,)), ((), ())), preferred_element_type=F32)


def left_lanes(shape):
    return lax.broadcasted_iota(jnp.int32, shape, len(shape) - 1) < HALF


def swap_halves(a):
    return pltpu.roll(a.astype(F32), HALF, a.ndim - 1).astype(a.dtype)


def tile_of(group):
    return 3 * (group // 2) + 2 * (group % 2)


def columns(tile):
    return pl.ds(pl.multiple_of(tile * 128, 128), 128)


def kernel(
    q_hbm, k_hbm, v_hbm, levels_hbm, plan_hbm, gate_hbm, fresh_hbm,
    den_ref, next_ref,
    levels_ref, plan_ref, index_sem,
    src, packed, gate_buf, gate_row,
    kt, vt, qt, kh, vh, qh,
    va, vb, ha, hb,
    ot, oh, ort, orh,
    in_sem, gate_sem,
    send_t, recv_t, send_h, recv_h,
    fwd_send_t, fwd_recv_t, fwd_send_h, fwd_recv_h,
    o_send_t, o_recv_t, o_send_h, o_recv_h,
    shift_send, shift_recv, fresh_sem,
    relay_buf, relay_send, relay_recv,
):
    queue = lax.axis_index("queue")
    space = lax.axis_index("space")
    z, y_lo, x = queue // 8, (queue // 4) % 2, queue % 4
    y_hi, core = space // 2, space % 2
    y = y_hi * 2 + y_lo
    frame = z * 8 + core * 4 + x
    nearer = 3 - 2 * y_lo
    near_pairs = [(y_hi + step) % 4 for step in (0, nearer, 4 - nearer, 2)]
    tokens_in = (kt, vt, qt)
    heads_in = (kh, vh, qh)

    def worker(of_frame, group):
        return (
            (of_frame // 8) * 8 + (group % 2) * 4 + of_frame % 4,
            (group // 2) * 2 + (of_frame // 4) % 2,
        )

    inputs = (k_hbm, v_hbm, q_hbm)
    loads = [
        pltpu.make_async_copy(ref.at[0], src.at[i], in_sem.at[i]) for i, ref in enumerate(inputs)
    ]
    gate_load = pltpu.make_async_copy(gate_hbm, gate_buf, gate_sem)

    for load in loads:
        load.start()
    gate_load.start()
    index_loads = [
        pltpu.make_async_copy(levels_hbm, levels_ref, index_sem.at[0]),
        pltpu.make_async_copy(plan_hbm, plan_ref, index_sem.at[1]),
    ]
    for load in index_loads:
        load.start()

    barrier = pltpu.get_barrier_semaphore()

    def greet(device):
        pl.semaphore_signal(barrier, inc=1, device_id=device, device_id_type=MESH)

    has_prev, has_next = frame > 0, frame < 63
    has_ahead, has_behind = queue > 0, queue < 63
    wraps = has_ahead & (x == 0)
    relays = (x > 0) & (queue - x > 0)
    owns = core == y_lo
    for i in range(8):
        @pl.when(jnp.logical_not(owns & (space == i)))
        def _():
            greet((frame, i))
    pl.when(has_prev)(lambda: greet(worker(frame - 1, y)))
    pl.when(has_behind)(lambda: greet((queue + 1, space)))

    @pl.when(has_behind & (x == 3))
    def _():
        for column in sorted(set(VIA)):
            greet((queue + 1 + column, space))

    for column in sorted(set(VIA)):
        pl.when(relays & (x == column))(lambda: greet((queue - x, space)))
    for i in range(GROUPS):
        @pl.when(jnp.logical_not(owns & (y == i)))
        def _():
            greet(worker(queue, i))
    greeted = (
        16
        - 2 * owns.astype(jnp.int32)
        + has_next.astype(jnp.int32)
        + has_ahead.astype(jnp.int32)
        + len(set(VIA)) * wraps.astype(jnp.int32)
        + sum((relays & (x == column)).astype(jnp.int32) for column in sorted(set(VIA)))
    )

    def pack(i):
        left = left_lanes((HALF, 128))
        for pair in range(4):
            tile = src[i, :, (3 * pair + 1) * 128 : (3 * pair + 2) * 128]
            top, bottom = tile[:HALF], tile[HALF:]
            packed[i, 2 * pair] = jnp.where(left, top, swap_halves(bottom))
            packed[i, 2 * pair + 1] = jnp.where(left, swap_halves(top), bottom)

    pl.semaphore_wait(barrier, greeted)

    def rows_of(index, size):
        return pl.ds(pl.multiple_of(index * size, size), size)

    def sent_tile(i, group):
        return pltpu.make_async_remote_copy(
            src_ref=src.at[i, :, columns(tile_of(group))],
            dst_ref=tokens_in[i].at[rows_of(space, ROWS)],
            send_sem=send_t.at[i, group], recv_sem=recv_t.at[i, space],
            device_id=worker(queue, group), device_id_type=MESH,
        )

    def sent_head(i, group):
        return pltpu.make_async_remote_copy(
            src_ref=packed.at[i, group],
            dst_ref=heads_in[i].at[rows_of(space, HALF)],
            send_sem=send_h.at[i, group], recv_sem=recv_h.at[i, space],
            device_id=worker(queue, group), device_id_type=MESH,
        )

    def send_out(make, kept, i, order=NEAR_FIRST):
        for shift in order:
            group = (y + shift) % GROUPS
            if shift:
                make(i, group).start()
            else:
                pl.when(owns)(lambda: kept(i).start())
                pl.when(jnp.logical_not(owns))(lambda: make(i, group).start())

    def kept_tile(i):
        return pltpu.make_async_copy(
            src.at[i, :, columns(tile_of(y))],
            tokens_in[i].at[rows_of(space, ROWS)],
            recv_t.at[i, space],
        )

    def kept_head(i):
        return pltpu.make_async_copy(
            packed.at[i, y],
            heads_in[i].at[rows_of(space, HALF)],
            recv_h.at[i, space],
        )

    with jax.named_scope("send_all"):
        for i in (K, V, Q):
            loads[i].wait()
            send_out(sent_tile, kept_tile, i)
            pack(i)
        for i in (K, V):
            send_out(sent_head, kept_head, i)

    def arrival_tile(i, shard):
        return pltpu.make_async_copy(
            tokens_in[i].at[rows_of(shard, ROWS)], tokens_in[i].at[rows_of(shard, ROWS)], recv_t.at[i, shard]
        )

    def arrival_head(i, shard):
        return pltpu.make_async_copy(
            heads_in[i].at[rows_of(shard, HALF)], heads_in[i].at[rows_of(shard, HALF)], recv_h.at[i, shard]
        )

    def forward(buf, i, pair, size, sends, recvs):
        return pltpu.make_async_remote_copy(
            src_ref=buf.at[rows_of(pair, 2 * size)],
            dst_ref=buf.at[rows_of(4 + pair, 2 * size)],
            send_sem=sends.at[i, pair], recv_sem=recvs.at[i, pair],
            device_id=worker(frame + 1, y), device_id_type=MESH,
        )

    def own_pair(arrival, i, pair):
        arrival(i, 2 * pair).wait()
        arrival(i, 2 * pair + 1).wait()

    def pass_on(i, arrival, buf, size, sends, recvs):
        for pair in near_pairs:
            own_pair(arrival, i, pair)
            pl.when(has_next)(lambda: forward(buf, i, pair, size, sends, recvs).start())

    def previous(i, buf, size, sends, recvs):
        @pl.when(has_prev)
        def _():
            for pair in range(4):
                forward(buf, i, pair, size, sends, recvs).wait_recv()

        if i == K:
            @pl.when(jnp.logical_not(has_prev))
            def _():
                half = 8 * size
                buf[pl.ds(half, half), :] = buf[pl.ds(0, half), :]

    def spread(buf, left_buf, right_buf, size):
        half = 8 * size
        left = left_lanes((half, 128))
        one = jnp.ones((), BF16)
        own = buf[pl.ds(0, half), :]
        left_buf[pl.ds(0, half), :] = jnp.where(left, own, one)
        right_buf[pl.ds(0, half), :] = jnp.where(left, one, own)

    def spread_previous(buf, left_buf, right_buf, size):
        half = 8 * size
        left = left_lanes((half, 128))
        one = jnp.ones((), BF16)

        @pl.when(has_prev)
        def _():
            before = buf[pl.ds(half, half), :]
            left_buf[pl.ds(half, half), :] = jnp.where(left, before, one)
            right_buf[pl.ds(half, half), :] = jnp.where(left, one, before)

        @pl.when(jnp.logical_not(has_prev))
        def _():
            left_buf[pl.ds(half, half), :] = jnp.zeros((half, 128), BF16)
            right_buf[pl.ds(half, half), :] = jnp.zeros((half, 128), BF16)

    def weights(scores):
        return jnp.exp(scores - jnp.max(scores, axis=1, keepdims=True)).astype(BF16)

    scale = jnp.asarray(0.125, BF16)
    zero = jnp.zeros((), BF16)

    def o_tile(shard):
        return pltpu.make_async_remote_copy(
            src_ref=ot.at[rows_of(shard, ROWS)], dst_ref=ort.at[rows_of(y, ROWS)],
            send_sem=o_send_t.at[shard], recv_sem=o_recv_t.at[y],
            device_id=(frame, shard), device_id_type=MESH,
        )

    def o_head(shard):
        return pltpu.make_async_remote_copy(
            src_ref=oh.at[rows_of(shard, HALF)], dst_ref=orh.at[rows_of(y, HALF)],
            send_sem=o_send_h.at[shard], recv_sem=o_recv_h.at[y],
            device_id=(frame, shard), device_id_type=MESH,
        )

    def o_out(make, buf, back, size, recvs, pair):
        for shard in (2 * pair, 2 * pair + 1):
            own = owns & (space == shard)
            @pl.when(own)
            def _():
                pltpu.make_async_copy(buf.at[rows_of(shard, size)], back.at[rows_of(y, size)], recvs.at[y]).start()
            @pl.when(jnp.logical_not(own))
            def _():
                make(shard).start()

    def attend_tile(pair):
        own_pair(arrival_tile, Q, pair)
        q = qt[rows_of(pair, 2 * ROWS), :] * scale
        left = left_lanes(q.shape)
        a = jnp.dot(weights(dot_nt(jnp.where(left, q, zero), kt[...])), va[...], preferred_element_type=F32)
        b = jnp.dot(weights(dot_nt(jnp.where(left, zero, q), kt[...])), vb[...], preferred_element_type=F32)
        top = jnp.where(left, a, b)
        total = pltpu.roll(jnp.where(left, b, a), HALF, 1)
        ot[rows_of(pair, 2 * ROWS), :] = (top / total).astype(BF16)
        o_out(o_tile, ot, ort, ROWS, o_recv_t, pair)

    def attend_heads(pairs):
        for pair in pairs:
            own_pair(arrival_head, Q, pair)
        keys = kh[...]
        for pair in pairs:
            q = qh[rows_of(pair, 2 * HALF), :] * scale
            turned = swap_halves(q)
            left = left_lanes(q.shape)
            q_left = jnp.concatenate([jnp.where(left, q, zero), jnp.where(left, turned, zero)], 0)
            q_right = jnp.concatenate([jnp.where(left, zero, turned), jnp.where(left, zero, q)], 0)
            w = weights(jnp.concatenate([dot_nt(q_left, keys), dot_nt(q_right, keys)], 1))
            a = jnp.dot(w[:, :1024], ha[...], preferred_element_type=F32)
            b = jnp.dot(w[:, 1024:], hb[...], preferred_element_type=F32)
            both = a + pltpu.roll(b, HALF, 1)
            mixed = both / pltpu.roll(both, HALF, 1)
            oh[rows_of(pair, 2 * HALF), :] = jnp.where(
                left, mixed[:ROWS], pltpu.roll(mixed[ROWS:], HALF, 1)
            ).astype(BF16)
        for pair in pairs:
            o_out(o_head, oh, orh, HALF, o_recv_h, pair)

    def shifted(tile):
        return pltpu.make_async_remote_copy(
            src_ref=den_ref.at[0, :, columns(tile)], dst_ref=next_ref.at[0, :, columns(tile)],
            send_sem=shift_send.at[tile], recv_sem=shift_recv.at[tile],
            device_id=(queue - 1, space), device_id_type=MESH,
        )

    def to_relay(tile, k):
        return pltpu.make_async_remote_copy(
            src_ref=den_ref.at[0, :, columns(tile)], dst_ref=relay_buf.at[k],
            send_sem=shift_send.at[tile], recv_sem=relay_recv.at[k],
            device_id=(queue + VIA[k], space), device_id_type=MESH,
        )

    def from_relay(tile, k):
        return pltpu.make_async_remote_copy(
            src_ref=relay_buf.at[k], dst_ref=next_ref.at[0, :, columns(tile)],
            send_sem=relay_send.at[k], recv_sem=shift_recv.at[tile],
            device_id=(queue - x - 1, space), device_id_type=MESH,
        )

    with jax.named_scope("wait_k"):
        pass_on(K, arrival_tile, kt, ROWS, fwd_send_t, fwd_recv_t)
    with jax.named_scope("wait_v"):
        pass_on(V, arrival_tile, vt, ROWS, fwd_send_t, fwd_recv_t)
    spread(vt, va, vb, ROWS)
    with jax.named_scope("wait_prev"):
        previous(K, kt, ROWS, fwd_send_t, fwd_recv_t)
        previous(V, vt, ROWS, fwd_send_t, fwd_recv_t)
    spread_previous(vt, va, vb, ROWS)
    for n, pair in enumerate(near_pairs):
        with jax.named_scope("attend_tile"):
            attend_tile(pair)
        if n == 0:
            send_out(sent_head, kept_head, Q, NEAR_FIRST[::-1])
        if n == 1:
            with jax.named_scope("wait_kh"):
                pass_on(K, arrival_head, kh, HALF, fwd_send_h, fwd_recv_h)
        if n == 2:
            with jax.named_scope("wait_vh"):
                pass_on(V, arrival_head, vh, HALF, fwd_send_h, fwd_recv_h)

    gate_load.wait()
    for load in index_loads:
        load.wait()
    step_now = plan_ref[levels_ref[0]]
    gate_row[...] = gate_buf[pl.ds(step_now, 1), :]

    def gated(tile, attn, k=len(VIA)):
        cut = columns(tile)
        den_ref[0, :, cut] = (gate_row[:, cut] * attn.astype(F32)).astype(BF16)
        if k < len(VIA):
            pl.when(has_ahead & (x > 0))(lambda: shifted(tile).start())
            pl.when(wraps)(lambda: to_relay(tile, k).start())
        else:
            pl.when(has_ahead)(lambda: shifted(tile).start())

    def arrived(back, index, size, recvs):
        pltpu.make_async_copy(
            back.at[rows_of(index, size)], back.at[rows_of(index, size)], recvs.at[index]
        ).wait()

    def finish_tile(k):
        group = tile_groups[k]
        arrived(ort, group, ROWS, o_recv_t)
        gated(tile_of(group), ort[rows_of(group, ROWS), :], k)

    def relay(act):
        for column in sorted(set(VIA)):
            @pl.when(relays & (x == column))
            def _():
                for k in range(len(VIA)):
                    if VIA[k] == column:
                        act(k)

    def pass_relayed(k):
        pltpu.make_async_copy(relay_buf.at[k], relay_buf.at[k], relay_recv.at[k]).wait()
        from_relay(tile_of(tile_groups[k]), k).start()

    def wait_relayed(k):
        from_relay(tile_of(tile_groups[k]), k).wait_send()

    def finish_heads(pair):
        left = left_lanes((HALF, 128))
        for group in (2 * pair, 2 * pair + 1):
            arrived(orh, group, HALF, o_recv_h)
        even = orh[rows_of(2 * pair, HALF), :]
        odd = orh[rows_of(2 * pair + 1, HALF), :]
        gated(
            3 * pair + 1,
            jnp.concatenate(
                [jnp.where(left, even, swap_halves(odd)), jnp.where(left, swap_halves(even), odd)], 0
            ),
        )

    with jax.named_scope("wait_prev_h"):
        spread(vh, ha, hb, HALF)
        previous(K, kh, HALF, fwd_send_h, fwd_recv_h)
        previous(V, vh, HALF, fwd_send_h, fwd_recv_h)
        spread_previous(vh, ha, hb, HALF)

    home = [(y_hi + step) % 4 for step in (0, 1, 3, 2)]
    tile_groups = [2 * home[0], 2 * home[0] + 1, 2 * home[1], 2 * home[2] + 1,
                   2 * home[2], 2 * home[1] + 1, 2 * home[3], 2 * home[3] + 1]
    for k in range(4):
        finish_tile(k)
    for pairs in (near_pairs[:1:-1], near_pairs[1::-1]):
        with jax.named_scope("attend_head"):
            attend_heads(pairs)
    with jax.named_scope("sent"):
        @pl.when(has_next)
        def _():
            for pair in range(4):
                for i, tiles, heads in ((K, kt, kh), (V, vt, vh)):
                    forward(tiles, i, pair, ROWS, fwd_send_t, fwd_recv_t).wait_send()
                    forward(heads, i, pair, HALF, fwd_send_h, fwd_recv_h).wait_send()

        for group in range(GROUPS):
            @pl.when(jnp.logical_not(owns & (group == y)))
            def _():
                for i in (K, V, Q):
                    sent_tile(i, group).wait_send()
                    sent_head(i, group).wait_send()
    with jax.named_scope("finish"):
        relay(pass_relayed)
        for k in range(4, 8):
            finish_tile(k)
        for shard in range(8):
            @pl.when(jnp.logical_not(owns & (space == shard)))
            def _():
                o_tile(shard).wait_send()
        for pair in home[::-1]:
            finish_heads(pair)
    @pl.when(jnp.logical_not(has_behind))
    def _():
        copy = pltpu.make_async_copy(fresh_hbm, next_ref.at[0], fresh_sem)
        copy.start()
        copy.wait()

    with jax.named_scope("wait_shift"):
        @pl.when(has_behind)
        def _():
            for tile in range(12):
                shifted(tile).wait_recv()

    with jax.named_scope("wait_sends"):
        relay(wait_relayed)

        @pl.when(has_ahead)
        def _():
            for tile in range(12):
                shifted(tile).wait_send()

        for shard in range(8):
            @pl.when(jnp.logical_not(owns & (space == shard)))
            def _():
                o_head(shard).wait_send()


def hand_over(den_ref, next_ref, den_out, next_out, sems):
    copies = [
        pltpu.make_async_copy(den_ref, den_out, sems.at[0]),
        pltpu.make_async_copy(next_ref, next_out, sems.at[1]),
    ]
    for copy in copies:
        copy.start()
    for copy in copies:
        copy.wait()


def body(queries, keys, values, levels, plan, gate_table, fresh):
    vmem = functools.partial(pltpu.VMEM, dtype=BF16)
    dma = lambda *shape: pltpu.SemaphoreType.DMA(shape)
    any_space = pl.BlockSpec(memory_space=pl.ANY)
    out = jax.ShapeDtypeStruct((1, ROWS, COLS), BF16)
    results = pl.pallas_call(
        kernel,
        out_shape=(out, out),
        in_specs=[any_space] * 3 + [pl.BlockSpec(memory_space=pltpu.HBM)] * 2 + [any_space] * 2,
        out_specs=[pl.BlockSpec(memory_space=pltpu.VMEM)] * 2,
        scratch_shapes=[
            pltpu.SMEM((1,), jnp.int32), pltpu.SMEM((64,), jnp.int32), dma(2),
            vmem((3, ROWS, COLS)), vmem((3, GROUPS, HALF, 128)), pltpu.VMEM((128, COLS), F32), pltpu.VMEM((1, COLS), F32),
            vmem((2048, 128)), vmem((2048, 128)), vmem((1024, 128)),
            vmem((1024, 128)), vmem((1024, 128)), vmem((512, 128)),
            vmem((2048, 128)), vmem((2048, 128)), vmem((1024, 128)), vmem((1024, 128)),
            vmem((1024, 128)), vmem((512, 128)), vmem((1024, 128)), vmem((512, 128)),
            dma(3), pltpu.SemaphoreType.DMA,
            dma(3, 8), dma(3, 8), dma(3, 8), dma(3, 8),
            dma(2, 4), dma(2, 4), dma(2, 4), dma(2, 4),
            dma(8), dma(8), dma(8), dma(8),
            dma(12), dma(12), pltpu.SemaphoreType.DMA,
            vmem((len(VIA), ROWS, 128)), dma(len(VIA)), dma(len(VIA)),
        ],
        compiler_params=pltpu.CompilerParams(
            collective_id=0, has_side_effects=True, vmem_limit_bytes=53 * 1024 * 1024
        ),
        name="frame_attention",
    )(queries, keys, values, levels, plan, gate_table, fresh)
    return pl.pallas_call(
        hand_over,
        out_shape=(out, out),
        in_specs=[pl.BlockSpec(memory_space=pl.ANY)] * 2,
        out_specs=[pl.BlockSpec(memory_space=pl.ANY)] * 2,
        scratch_shapes=[dma(2)],
        compiler_params=pltpu.CompilerParams(vmem_limit_bytes=8 * 1024 * 1024),
        name="hand_over",
    )(*results)


def solution(mesh):
    return jax.shard_map(
        body,
        mesh=mesh,
        in_specs=(
            P("queue", "space", None),
            P("queue", "space", None),
            P("queue", "space", None),
            P("queue"),
            P(),
            P(),
            P("space", None),
        ),
        out_specs=(P("queue", "space", None), P("queue", "space", None)),
        check_vma=False,
    )
```

```python
import functools

import jax
import jax.numpy as jnp
from jax import lax
from jax.experimental import pallas as pl
from jax.experimental.pallas import tpu as pltpu
from jax.sharding import PartitionSpec as P

MESH = pl.DeviceIdType.MESH
BF16 = jnp.bfloat16
F32 = jnp.float32
ROWS = 128
HALF = 64
COLS = 1536
GROUPS = 8
NEAR_FIRST = (0, 1, 7, 2, 6, 3, 5, 4)
K, V, Q = 0, 1, 2
VIA = (3, 1, 2, 3)


def dot_nt(a, b):
    return lax.dot_general(a, b, (((1,), (1,)), ((), ())), preferred_element_type=F32)


def left_lanes(shape):
    return lax.broadcasted_iota(jnp.int32, shape, len(shape) - 1) < HALF


def swap_halves(a):
    return pltpu.roll(a.astype(F32), HALF, a.ndim - 1).astype(a.dtype)


def tile_of(group):
    return 3 * (group // 2) + 2 * (group % 2)


def columns(tile):
    return pl.ds(pl.multiple_of(tile * 128, 128), 128)


def kernel(
    q_hbm, k_hbm, v_hbm, levels_hbm, plan_hbm, gate_hbm, fresh_hbm,
    den_ref, next_ref,
    levels_ref, plan_ref, index_sem,
    src, packed, gate_buf, gate_row,
    kt, vt, qt, kh, vh, qh,
    va, vb, ha, hb,
    ot, oh, ort, orh,
    in_sem, gate_sem,
    send_t, recv_t, send_h, recv_h,
    fwd_send_t, fwd_recv_t, fwd_send_h, fwd_recv_h,
    o_send_t, o_recv_t, o_send_h, o_recv_h,
    shift_send, shift_recv, fresh_sem,
    relay_buf, relay_send, relay_recv,
):
    queue = lax.axis_index("queue")
    space = lax.axis_index("space")
    z, y_lo, x = queue // 8, (queue // 4) % 2, queue % 4
    y_hi, core = space // 2, space % 2
    y = y_hi * 2 + y_lo
    frame = z * 8 + core * 4 + x
    nearer = 3 - 2 * y_lo
    near_pairs = [(y_hi + step) % 4 for step in (0, nearer, 4 - nearer, 2)]
    tokens_in = (kt, vt, qt)
    heads_in = (kh, vh, qh)

    def worker(of_frame, group):
        return (
            (of_frame // 8) * 8 + (group % 2) * 4 + of_frame % 4,
            (group // 2) * 2 + (of_frame // 4) % 2,
        )

    inputs = (k_hbm, v_hbm, q_hbm)
    loads = [
        pltpu.make_async_copy(ref.at[0], src.at[i], in_sem.at[i]) for i, ref in enumerate(inputs)
    ]
    gate_load = pltpu.make_async_copy(gate_hbm, gate_buf, gate_sem)

    for load in loads:
        load.start()
    gate_load.start()
    index_loads = [
        pltpu.make_async_copy(levels_hbm, levels_ref, index_sem.at[0]),
        pltpu.make_async_copy(plan_hbm, plan_ref, index_sem.at[1]),
    ]
    for load in index_loads:
        load.start()

    barrier = pltpu.get_barrier_semaphore()

    def greet(device):
        pl.semaphore_signal(barrier, inc=1, device_id=device, device_id_type=MESH)

    has_prev, has_next = frame > 0, frame < 63
    has_ahead, has_behind = queue > 0, queue < 63
    wraps = has_ahead & (x == 0)
    relays = (x > 0) & (queue - x > 0)
    owns = core == y_lo
    for i in range(8):
        @pl.when(jnp.logical_not(owns & (space == i)))
        def _():
            greet((frame, i))
    pl.when(has_prev)(lambda: greet(worker(frame - 1, y)))
    pl.when(has_behind)(lambda: greet((queue + 1, space)))

    @pl.when(has_behind & (x == 3))
    def _():
        for column in sorted(set(VIA)):
            greet((queue + 1 + column, space))

    for column in sorted(set(VIA)):
        pl.when(relays & (x == column))(lambda: greet((queue - x, space)))
    for i in range(GROUPS):
        @pl.when(jnp.logical_not(owns & (y == i)))
        def _():
            greet(worker(queue, i))
    greeted = (
        16
        - 2 * owns.astype(jnp.int32)
        + has_next.astype(jnp.int32)
        + has_ahead.astype(jnp.int32)
        + len(set(VIA)) * wraps.astype(jnp.int32)
        + sum((relays & (x == column)).astype(jnp.int32) for column in sorted(set(VIA)))
    )

    def pack(i):
        left = left_lanes((HALF, 128))
        for pair in range(4):
            tile = src[i, :, (3 * pair + 1) * 128 : (3 * pair + 2) * 128]
            top, bottom = tile[:HALF], tile[HALF:]
            packed[i, 2 * pair] = jnp.where(left, top, swap_halves(bottom))
            packed[i, 2 * pair + 1] = jnp.where(left, swap_halves(top), bottom)

    pl.semaphore_wait(barrier, greeted)

    def rows_of(index, size):
        return pl.ds(pl.multiple_of(index * size, size), size)

    def sent_tile(i, group):
        return pltpu.make_async_remote_copy(
            src_ref=src.at[i, :, columns(tile_of(group))],
            dst_ref=tokens_in[i].at[rows_of(space, ROWS)],
            send_sem=send_t.at[i, group], recv_sem=recv_t.at[i, space],
            device_id=worker(queue, group), device_id_type=MESH,
        )

    def sent_head(i, group):
        return pltpu.make_async_remote_copy(
            src_ref=packed.at[i, group],
            dst_ref=heads_in[i].at[rows_of(space, HALF)],
            send_sem=send_h.at[i, group], recv_sem=recv_h.at[i, space],
            device_id=worker(queue, group), device_id_type=MESH,
        )

    def send_out(make, kept, i, order=NEAR_FIRST):
        for shift in order:
            group = (y + shift) % GROUPS
            if shift:
                make(i, group).start()
            else:
                pl.when(owns)(lambda: kept(i).start())
                pl.when(jnp.logical_not(owns))(lambda: make(i, group).start())

    def kept_tile(i):
        return pltpu.make_async_copy(
            src.at[i, :, columns(tile_of(y))],
            tokens_in[i].at[rows_of(space, ROWS)],
            recv_t.at[i, space],
        )

    def kept_head(i):
        return pltpu.make_async_copy(
            packed.at[i, y],
            heads_in[i].at[rows_of(space, HALF)],
            recv_h.at[i, space],
        )

    with jax.named_scope("send_all"):
        for i in (K, V, Q):
            loads[i].wait()
            send_out(sent_tile, kept_tile, i)
            pack(i)
        for i in (K, V):
            send_out(sent_head, kept_head, i)

    def arrival_tile(i, shard):
        return pltpu.make_async_copy(
            tokens_in[i].at[rows_of(shard, ROWS)], tokens_in[i].at[rows_of(shard, ROWS)], recv_t.at[i, shard]
        )

    def arrival_head(i, shard):
        return pltpu.make_async_copy(
            heads_in[i].at[rows_of(shard, HALF)], heads_in[i].at[rows_of(shard, HALF)], recv_h.at[i, shard]
        )

    def forward(buf, i, pair, size, sends, recvs):
        return pltpu.make_async_remote_copy(
            src_ref=buf.at[rows_of(pair, 2 * size)],
            dst_ref=buf.at[rows_of(4 + pair, 2 * size)],
            send_sem=sends.at[i, pair], recv_sem=recvs.at[i, pair],
            device_id=worker(frame + 1, y), device_id_type=MESH,
        )

    def own_pair(arrival, i, pair):
        arrival(i, 2 * pair).wait()
        arrival(i, 2 * pair + 1).wait()

    def pass_on(i, arrival, buf, size, sends, recvs):
        for pair in near_pairs:
            own_pair(arrival, i, pair)
            pl.when(has_next)(lambda: forward(buf, i, pair, size, sends, recvs).start())

    def previous(i, buf, size, sends, recvs):
        @pl.when(has_prev)
        def _():
            for pair in range(4):
                forward(buf, i, pair, size, sends, recvs).wait_recv()

        if i == K:
            @pl.when(jnp.logical_not(has_prev))
            def _():
                half = 8 * size
                buf[pl.ds(half, half), :] = buf[pl.ds(0, half), :]

    def spread(buf, left_buf, right_buf, size):
        half = 8 * size
        left = left_lanes((half, 128))
        one = jnp.ones((), BF16)
        own = buf[pl.ds(0, half), :]
        left_buf[pl.ds(0, half), :] = jnp.where(left, own, one)
        right_buf[pl.ds(0, half), :] = jnp.where(left, one, own)

    def spread_previous(buf, left_buf, right_buf, size):
        half = 8 * size
        left = left_lanes((half, 128))
        one = jnp.ones((), BF16)

        @pl.when(has_prev)
        def _():
            before = buf[pl.ds(half, half), :]
            left_buf[pl.ds(half, half), :] = jnp.where(left, before, one)
            right_buf[pl.ds(half, half), :] = jnp.where(left, one, before)

        @pl.when(jnp.logical_not(has_prev))
        def _():
            left_buf[pl.ds(half, half), :] = jnp.zeros((half, 128), BF16)
            right_buf[pl.ds(half, half), :] = jnp.zeros((half, 128), BF16)

    def weights(scores):
        return jnp.exp(scores - jnp.max(scores, axis=1, keepdims=True)).astype(BF16)

    scale = jnp.asarray(0.125, BF16)
    zero = jnp.zeros((), BF16)

    def o_tile(shard):
        return pltpu.make_async_remote_copy(
            src_ref=ot.at[rows_of(shard, ROWS)], dst_ref=ort.at[rows_of(y, ROWS)],
            send_sem=o_send_t.at[shard], recv_sem=o_recv_t.at[y],
            device_id=(frame, shard), device_id_type=MESH,
        )

    def o_head(shard):
        return pltpu.make_async_remote_copy(
            src_ref=oh.at[rows_of(shard, HALF)], dst_ref=orh.at[rows_of(y, HALF)],
            send_sem=o_send_h.at[shard], recv_sem=o_recv_h.at[y],
            device_id=(frame, shard), device_id_type=MESH,
        )

    def o_out(make, buf, back, size, recvs, pair):
        for shard in (2 * pair, 2 * pair + 1):
            own = owns & (space == shard)
            @pl.when(own)
            def _():
                pltpu.make_async_copy(buf.at[rows_of(shard, size)], back.at[rows_of(y, size)], recvs.at[y]).start()
            @pl.when(jnp.logical_not(own))
            def _():
                make(shard).start()

    def attend_tile(pair):
        own_pair(arrival_tile, Q, pair)
        q = qt[rows_of(pair, 2 * ROWS), :] * scale
        left = left_lanes(q.shape)
        a = jnp.dot(weights(dot_nt(jnp.where(left, q, zero), kt[...])), va[...], preferred_element_type=F32)
        b = jnp.dot(weights(dot_nt(jnp.where(left, zero, q), kt[...])), vb[...], preferred_element_type=F32)
        top = jnp.where(left, a, b)
        total = pltpu.roll(jnp.where(left, b, a), HALF, 1)
        ot[rows_of(pair, 2 * ROWS), :] = (top / total).astype(BF16)
        o_out(o_tile, ot, ort, ROWS, o_recv_t, pair)

    def attend_heads(pairs):
        for pair in pairs:
            own_pair(arrival_head, Q, pair)
        keys = kh[...]
        for pair in pairs:
            q = qh[rows_of(pair, 2 * HALF), :] * scale
            turned = swap_halves(q)
            left = left_lanes(q.shape)
            q_left = jnp.concatenate([jnp.where(left, q, zero), jnp.where(left, turned, zero)], 0)
            q_right = jnp.concatenate([jnp.where(left, zero, turned), jnp.where(left, zero, q)], 0)
            w = weights(jnp.concatenate([dot_nt(q_left, keys), dot_nt(q_right, keys)], 1))
            a = jnp.dot(w[:, :1024], ha[...], preferred_element_type=F32)
            b = jnp.dot(w[:, 1024:], hb[...], preferred_element_type=F32)
            both = a + pltpu.roll(b, HALF, 1)
            mixed = both / pltpu.roll(both, HALF, 1)
            oh[rows_of(pair, 2 * HALF), :] = jnp.where(
                left, mixed[:ROWS], pltpu.roll(mixed[ROWS:], HALF, 1)
            ).astype(BF16)
        for pair in pairs:
            o_out(o_head, oh, orh, HALF, o_recv_h, pair)

    def shifted(tile):
        return pltpu.make_async_remote_copy(
            src_ref=den_ref.at[0, :, columns(tile)], dst_ref=next_ref.at[0, :, columns(tile)],
            send_sem=shift_send.at[tile], recv_sem=shift_recv.at[tile],
            device_id=(queue - 1, space), device_id_type=MESH,
        )

    def to_relay(tile, k):
        return pltpu.make_async_remote_copy(
            src_ref=den_ref.at[0, :, columns(tile)], dst_ref=relay_buf.at[k],
            send_sem=shift_send.at[tile], recv_sem=relay_recv.at[k],
            device_id=(queue + VIA[k], space), device_id_type=MESH,
        )

    def from_relay(tile, k):
        return pltpu.make_async_remote_copy(
            src_ref=relay_buf.at[k], dst_ref=next_ref.at[0, :, columns(tile)],
            send_sem=relay_send.at[k], recv_sem=shift_recv.at[tile],
            device_id=(queue - x - 1, space), device_id_type=MESH,
        )

    with jax.named_scope("wait_k"):
        pass_on(K, arrival_tile, kt, ROWS, fwd_send_t, fwd_recv_t)
    with jax.named_scope("wait_v"):
        pass_on(V, arrival_tile, vt, ROWS, fwd_send_t, fwd_recv_t)
    spread(vt, va, vb, ROWS)
    with jax.named_scope("wait_prev"):
        previous(K, kt, ROWS, fwd_send_t, fwd_recv_t)
        previous(V, vt, ROWS, fwd_send_t, fwd_recv_t)
    spread_previous(vt, va, vb, ROWS)
    for n, pair in enumerate(near_pairs):
        with jax.named_scope("attend_tile"):
            attend_tile(pair)
        if n == 0:
            send_out(sent_head, kept_head, Q, NEAR_FIRST[::-1])
        if n == 1:
            with jax.named_scope("wait_kh"):
                pass_on(K, arrival_head, kh, HALF, fwd_send_h, fwd_recv_h)
        if n == 2:
            with jax.named_scope("wait_vh"):
                pass_on(V, arrival_head, vh, HALF, fwd_send_h, fwd_recv_h)

    gate_load.wait()
    for load in index_loads:
        load.wait()
    step_now = plan_ref[levels_ref[0]]
    gate_row[...] = gate_buf[pl.ds(step_now, 1), :]

    def gated(tile, attn, k=len(VIA)):
        cut = columns(tile)
        den_ref[0, :, cut] = (gate_row[:, cut] * attn.astype(F32)).astype(BF16)
        if k < len(VIA):
            pl.when(has_ahead & (x > 0))(lambda: shifted(tile).start())
            pl.when(wraps)(lambda: to_relay(tile, k).start())
        else:
            pl.when(has_ahead)(lambda: shifted(tile).start())

    def arrived(back, index, size, recvs):
        pltpu.make_async_copy(
            back.at[rows_of(index, size)], back.at[rows_of(index, size)], recvs.at[index]
        ).wait()

    def finish_tile(k):
        group = tile_groups[k]
        arrived(ort, group, ROWS, o_recv_t)
        gated(tile_of(group), ort[rows_of(group, ROWS), :], k)

    def relay(act):
        for column in sorted(set(VIA)):
            @pl.when(relays & (x == column))
            def _():
                for k in range(len(VIA)):
                    if VIA[k] == column:
                        act(k)

    def pass_relayed(k):
        pltpu.make_async_copy(relay_buf.at[k], relay_buf.at[k], relay_recv.at[k]).wait()
        from_relay(tile_of(tile_groups[k]), k).start()

    def wait_relayed(k):
        from_relay(tile_of(tile_groups[k]), k).wait_send()

    def finish_heads(pair):
        left = left_lanes((HALF, 128))
        for group in (2 * pair, 2 * pair + 1):
            arrived(orh, group, HALF, o_recv_h)
        even = orh[rows_of(2 * pair, HALF), :]
        odd = orh[rows_of(2 * pair + 1, HALF), :]
        gated(
            3 * pair + 1,
            jnp.concatenate(
                [jnp.where(left, even, swap_halves(odd)), jnp.where(left, swap_halves(even), odd)], 0
            ),
        )

    with jax.named_scope("wait_prev_h"):
        spread(vh, ha, hb, HALF)
        previous(K, kh, HALF, fwd_send_h, fwd_recv_h)
        previous(V, vh, HALF, fwd_send_h, fwd_recv_h)
        spread_previous(vh, ha, hb, HALF)

    home = [(y_hi + step) % 4 for step in (0, 1, 3, 2)]
    tile_groups = [2 * home[0], 2 * home[0] + 1, 2 * home[1], 2 * home[2] + 1,
                   2 * home[2], 2 * home[1] + 1, 2 * home[3], 2 * home[3] + 1]
    for k in range(2):
        finish_tile(k)
    for n, pairs in enumerate((near_pairs[:1:-1], near_pairs[1::-1])):
        with jax.named_scope("attend_head"):
            attend_heads(pairs)
        if n == 0:
            for k in range(2, 4):
                finish_tile(k)
    with jax.named_scope("sent"):
        @pl.when(has_next)
        def _():
            for pair in range(4):
                for i, tiles, heads in ((K, kt, kh), (V, vt, vh)):
                    forward(tiles, i, pair, ROWS, fwd_send_t, fwd_recv_t).wait_send()
                    forward(heads, i, pair, HALF, fwd_send_h, fwd_recv_h).wait_send()

        for group in range(GROUPS):
            @pl.when(jnp.logical_not(owns & (group == y)))
            def _():
                for i in (K, V, Q):
                    sent_tile(i, group).wait_send()
                    sent_head(i, group).wait_send()
    with jax.named_scope("finish"):
        relay(pass_relayed)
        for k in range(4, 8):
            finish_tile(k)
        for shard in range(8):
            @pl.when(jnp.logical_not(owns & (space == shard)))
            def _():
                o_tile(shard).wait_send()
        for pair in home[::-1]:
            finish_heads(pair)
    @pl.when(jnp.logical_not(has_behind))
    def _():
        copy = pltpu.make_async_copy(fresh_hbm, next_ref.at[0], fresh_sem)
        copy.start()
        copy.wait()

    with jax.named_scope("wait_shift"):
        @pl.when(has_behind)
        def _():
            for tile in range(12):
                shifted(tile).wait_recv()

    with jax.named_scope("wait_sends"):
        relay(wait_relayed)

        @pl.when(has_ahead)
        def _():
            for tile in range(12):
                shifted(tile).wait_send()

        for shard in range(8):
            @pl.when(jnp.logical_not(owns & (space == shard)))
            def _():
                o_head(shard).wait_send()


def hand_over(den_ref, next_ref, den_out, next_out, sems):
    copies = [
        pltpu.make_async_copy(den_ref, den_out, sems.at[0]),
        pltpu.make_async_copy(next_ref, next_out, sems.at[1]),
    ]
    for copy in copies:
        copy.start()
    for copy in copies:
        copy.wait()


def body(queries, keys, values, levels, plan, gate_table, fresh):
    vmem = functools.partial(pltpu.VMEM, dtype=BF16)
    dma = lambda *shape: pltpu.SemaphoreType.DMA(shape)
    any_space = pl.BlockSpec(memory_space=pl.ANY)
    out = jax.ShapeDtypeStruct((1, ROWS, COLS), BF16)
    results = pl.pallas_call(
        kernel,
        out_shape=(out, out),
        in_specs=[any_space] * 3 + [pl.BlockSpec(memory_space=pltpu.HBM)] * 2 + [any_space] * 2,
        out_specs=[pl.BlockSpec(memory_space=pltpu.VMEM)] * 2,
        scratch_shapes=[
            pltpu.SMEM((1,), jnp.int32), pltpu.SMEM((64,), jnp.int32), dma(2),
            vmem((3, ROWS, COLS)), vmem((3, GROUPS, HALF, 128)), pltpu.VMEM((128, COLS), F32), pltpu.VMEM((1, COLS), F32),
            vmem((2048, 128)), vmem((2048, 128)), vmem((1024, 128)),
            vmem((1024, 128)), vmem((1024, 128)), vmem((512, 128)),
            vmem((2048, 128)), vmem((2048, 128)), vmem((1024, 128)), vmem((1024, 128)),
            vmem((1024, 128)), vmem((512, 128)), vmem((1024, 128)), vmem((512, 128)),
            dma(3), pltpu.SemaphoreType.DMA,
            dma(3, 8), dma(3, 8), dma(3, 8), dma(3, 8),
            dma(2, 4), dma(2, 4), dma(2, 4), dma(2, 4),
            dma(8), dma(8), dma(8), dma(8),
            dma(12), dma(12), pltpu.SemaphoreType.DMA,
            vmem((len(VIA), ROWS, 128)), dma(len(VIA)), dma(len(VIA)),
        ],
        compiler_params=pltpu.CompilerParams(
            collective_id=0, has_side_effects=True, vmem_limit_bytes=53 * 1024 * 1024
        ),
        name="frame_attention",
    )(queries, keys, values, levels, plan, gate_table, fresh)
    return pl.pallas_call(
        hand_over,
        out_shape=(out, out),
        in_specs=[pl.BlockSpec(memory_space=pl.ANY)] * 2,
        out_specs=[pl.BlockSpec(memory_space=pl.ANY)] * 2,
        scratch_shapes=[dma(2)],
        compiler_params=pltpu.CompilerParams(vmem_limit_bytes=8 * 1024 * 1024),
        name="hand_over",
    )(*results)


def solution(mesh):
    return jax.shard_map(
        body,
        mesh=mesh,
        in_specs=(
            P("queue", "space", None),
            P("queue", "space", None),
            P("queue", "space", None),
            P("queue"),
            P(),
            P(),
            P("space", None),
        ),
        out_specs=(P("queue", "space", None), P("queue", "space", None)),
        check_vma=False,
    )
```
